128 devices in a mesh: dp: 16 (over z, x_hi, core), mp: 8 (over y, x_lo).
Axes of the slice: x: 4 (x_hi: 2, x_lo: 2; x = x_hi * 2 + x_lo), y: 4, z: 4, core: 2. Of those that a mesh axis runs over, the one named last changes fastest.
Arguments:
- tokens: bfloat16 [12288, 2048], P('dp'), may hold values from -20 to 20
- cotangent: bfloat16 [12288, 2048], P('dp'), may hold values from -6 to 6
- w_gate: bfloat16 [2048, 8192], P(None, 'mp'), may hold values from -1 to 1
- w_up: bfloat16 [2048, 8192], P(None, 'mp'), may hold values from -1 to 1
- w_down: bfloat16 [8192, 2048], P('mp'), may hold values from -0.0625 to 0.0625
- row_gate: float32 [2048], P('dp'), may hold values from 0.0003 to 20
- col_gate: float32 [8192], P('mp'), may hold values from 0.0003 to 10
- row_up: float32 [2048], P('dp'), may hold values from 0.0003 to 20
- col_up: float32 [8192], P('mp'), may hold values from 0.0003 to 10
- row_down: float32 [8192], P(('mp', 'dp')), may hold values from 0.01 to 300
- col_down: float32 [2048], replicated, may hold values from 0.01 to 300
Outputs:
- token_grad: bfloat16 [12288, 2048], P('dp', 'mp')
- update_gate: float32 [2048, 8192], P('dp', 'mp')
- update_up: float32 [2048, 8192], P('dp', 'mp')
- update_down: float32 [8192, 2048], P(('mp', 'dp'))
- row_gate_new: float32 [2048], P('dp')
- col_gate_new: float32 [8192], P('mp')
- row_up_new: float32 [2048], P('dp')
- col_up_new: float32 [8192], P('mp')
- row_down_new: float32 [8192], P(('mp', 'dp'))
- col_down_new: float32 [2048], replicated
The draws below stay inside these ranges and needn't reach their ends.
All inputs are finite; a program needn't handle non-finite values.
Results may differ from the reference program's by a relative error of at most 0.015.
Values may be sent and summed in bfloat16 or wider, within the bound.
No kernel may reach another device: no remote copies, remote signals or barrier semaphores. Data moves between devices by JAX's collectives and lax.ppermute only.
A program may use at most 128 MiB of HBM per device.

```python
import jax
import jax.numpy as jnp
from jax import lax

D = 2048
FF = 8192
TOK_DEV = 768
TOKENS = 12288
N_DP = 16
N_MP = 8


def half_pattern(row_count, col_count, match_value, other_value):
    row_first = jnp.arange(row_count) < row_count // 2
    col_first = jnp.arange(col_count) < col_count // 2
    return jnp.where(row_first[:, None] == col_first[None, :], match_value, other_value).astype(jnp.float32)


def split_levels(key, length_all, first_low, first_high, second_low, second_high):
    fraction = jax.random.uniform(key, (length_all,), jnp.float32)
    first_half = jnp.arange(length_all) < length_all // 2
    low_end = jnp.log(jnp.where(first_half, first_low, second_low))
    high_end = jnp.log(jnp.where(first_half, first_high, second_high))
    return jnp.exp(low_end + fraction * (high_end - low_end)).astype(jnp.float32)


def draw_tokens(key, part):
    key = jax.random.fold_in(key, 11)
    base_key, jitter_key = jax.random.split(key)
    half_position = (jnp.arange(D) % (D // 2)).astype(jnp.float32) / (D // 2)
    base_values = jax.random.truncated_normal(base_key, -4.0, 4.0, (TOKENS, D), jnp.float32)
    spread = jnp.log(10.0)
    jitter = jax.random.uniform(jitter_key, (D,), jnp.float32, -0.35, 0.35)
    column_scale = jnp.exp(spread * (half_position - 1.0) + jitter)
    emphasis = half_pattern(TOKENS, D, 3.0, 1.0 / 3.0)
    return (base_values * column_scale[None, :] * emphasis).astype(jnp.bfloat16)


def draw_cotangent(key, part):
    key = jax.random.fold_in(key, 12)
    base_values = jax.random.truncated_normal(key, -4.0, 4.0, (TOKENS, D), jnp.float32)
    emphasis = half_pattern(TOKENS, D, 1.5, 0.5 / 3.0)
    return (base_values * emphasis).astype(jnp.bfloat16)


def draw_w_gate(key, part):
    key = jax.random.fold_in(key, 13)
    base_values = jax.random.truncated_normal(key, -4.0, 4.0, (D, FF), jnp.float32)
    levels = half_pattern(D, FF, 2.0, 0.5)
    return (base_values * levels * float(D) ** (-0.5)).astype(jnp.bfloat16)


def draw_w_up(key, part):
    key = jax.random.fold_in(key, 14)
    base_values = jax.random.truncated_normal(key, -4.0, 4.0, (D, FF), jnp.float32)
    levels = half_pattern(D, FF, 2.0, 0.5)
    return (base_values * levels * float(D) ** (-0.5)).astype(jnp.bfloat16)


def draw_row_gate(key, part):
    key = jax.random.fold_in(key, 21)
    return split_levels(key, D, 1.0, 2.0, 0.0003, 0.001)


def draw_col_gate(key, part):
    key = jax.random.fold_in(key, 22)
    return split_levels(key, FF, 0.0003, 0.001, 1.0, 2.0)


def draw_row_up(key, part):
    key = jax.random.fold_in(key, 23)
    return split_levels(key, D, 1.0, 2.0, 0.0003, 0.001)


def draw_col_up(key, part):
    key = jax.random.fold_in(key, 24)
    return split_levels(key, FF, 0.0003, 0.001, 1.0, 2.0)


def draw_row_down(key, part):
    key = jax.random.fold_in(key, 25)
    return split_levels(key, FF, 30.0, 60.0, 0.01, 0.03)


def draw_col_down(key, part):
    key = jax.random.fold_in(key, 26)
    return split_levels(key, D, 0.01, 0.03, 30.0, 60.0)


def block_scale(stream_key, shape, cuts, low, largest):
    factor_of, own = 1.0, jax.random.fold_in(stream_key, 6)
    for dim, blocks in cuts:
        steps = jnp.exp(jax.random.uniform(jax.random.fold_in(own, dim), (blocks,), jnp.float32, low / len(cuts), largest / len(cuts)))
        factor_of = factor_of * jnp.repeat(steps, shape[dim] // blocks).reshape([-1 if axis == dim else 1 for axis in range(len(shape))])
    return factor_of


def bell_draw(stream_key, dims, deviation, reach, pieces=(), dtype=jnp.bfloat16):
    array = jax.random.normal(stream_key, dims, jnp.float32) * deviation
    if len(pieces) > 0:
        array = block_scale(stream_key, dims, pieces, -0.22, 0.18) * array
    return jnp.clip(array, min=-reach, max=reach).astype(dtype)


def setup_inputs(seed: int = 0) -> dict:
    seeds = jax.random.split(jax.random.key(seed), 12)
    tokens = draw_tokens(jax.random.fold_in(seeds[11], 71), 0)
    cotangent = draw_cotangent(jax.random.fold_in(seeds[11], 71), 0)
    w_gate = draw_w_gate(jax.random.fold_in(seeds[11], 71), 0)
    w_up = draw_w_up(jax.random.fold_in(seeds[11], 71), 0)
    w_down = bell_draw(seeds[4], (FF, D), FF ** -0.5, 0.0625, ((0, 8),))
    row_gate = draw_row_gate(jax.random.fold_in(seeds[11], 71), 0)
    col_gate = draw_col_gate(jax.random.fold_in(seeds[11], 71), 0)
    row_up = draw_row_up(jax.random.fold_in(seeds[11], 71), 0)
    col_up = draw_col_up(jax.random.fold_in(seeds[11], 71), 0)
    row_down = draw_row_down(jax.random.fold_in(seeds[11], 71), 0)
    col_down = draw_col_down(jax.random.fold_in(seeds[11], 71), 0)
    return dict(tokens=tokens, cotangent=cotangent, w_gate=w_gate, w_up=w_up, w_down=w_down, row_gate=row_gate, col_gate=col_gate, row_up=row_up, col_up=col_up, row_down=row_down, col_down=col_down)


epsilon_one = 1e-30
decay_rate = 0.8

def silu_parts(gate_pre):
    sig = jax.nn.sigmoid(gate_pre)
    return (gate_pre * sig, sig * (1.0 + gate_pre * (1.0 - sig)))

def factored(grad, row_old, col_old):
    squares = grad * grad
    row_new = decay_rate * row_old + (1.0 - decay_rate) * (lax.optimization_barrier(jnp.mean(squares, 1)) + epsilon_one)
    col_new = decay_rate * col_old + (1.0 - decay_rate) * (lax.optimization_barrier(jnp.mean(squares, 0)) + epsilon_one)
    second = row_new[:, None] * col_new[None, :] / jnp.mean(row_new)
    raw = grad / jnp.sqrt(second)
    rms_value = jnp.sqrt(jnp.mean(raw * raw))
    return (raw / jnp.maximum(1.0, rms_value), row_new, col_new)

def reference(tokens, cotangent, w_gate, w_up, w_down, row_gate, col_gate, row_up, col_up, row_down, col_down):
    gate_pre = jnp.dot(tokens, w_gate, preferred_element_type=jnp.float32)
    up_pre = jnp.dot(tokens, w_up, preferred_element_type=jnp.float32)
    activated, derivative = silu_parts(gate_pre)
    hidden = (activated * up_pre).astype(jnp.bfloat16)
    hidden_grad = jnp.dot(cotangent, w_down.T, preferred_element_type=jnp.float32)
    grad_gate = (hidden_grad * up_pre * derivative).astype(jnp.bfloat16)
    grad_up = (hidden_grad * activated).astype(jnp.bfloat16)
    block_units = FF // N_MP
    token_total = jnp.zeros((TOKENS, D), jnp.float32)
    for block in range(N_MP):
        lower = block * block_units
        upper = lower + block_units
        partial_sum = jnp.dot(grad_gate[:, lower:upper], w_gate[:, lower:upper].T, preferred_element_type=jnp.float32)
        partial_sum = partial_sum + jnp.dot(grad_up[:, lower:upper], w_up[:, lower:upper].T, preferred_element_type=jnp.float32)
        rounded = lax.optimization_barrier(partial_sum.astype(jnp.bfloat16))
        token_total = token_total + rounded.astype(jnp.float32)
    token_grad = token_total.astype(jnp.bfloat16)
    grad_scale = float(TOKENS) ** (-0.5)
    g_gate = jnp.zeros((D, FF), jnp.float32)
    g_up = jnp.zeros((D, FF), jnp.float32)
    g_down = jnp.zeros((FF, D), jnp.float32)
    for block in range(N_DP):
        lower = block * TOK_DEV
        upper = lower + TOK_DEV
        term_gate = jnp.dot(tokens[lower:upper].T, grad_gate[lower:upper], preferred_element_type=jnp.float32) * grad_scale
        term_up = jnp.dot(tokens[lower:upper].T, grad_up[lower:upper], preferred_element_type=jnp.float32) * grad_scale
        term_down = jnp.dot(hidden[lower:upper].T, cotangent[lower:upper], preferred_element_type=jnp.float32) * grad_scale
        g_gate = g_gate + lax.optimization_barrier(term_gate.astype(jnp.bfloat16)).astype(jnp.float32)
        g_up = g_up + lax.optimization_barrier(term_up.astype(jnp.bfloat16)).astype(jnp.float32)
        g_down = g_down + lax.optimization_barrier(term_down.astype(jnp.bfloat16)).astype(jnp.float32)
    update_gate, row_gate_new, col_gate_new = factored(g_gate, row_gate, col_gate)
    update_up, row_up_new, col_up_new = factored(g_up, row_up, col_up)
    update_down, row_down_new, col_down_new = factored(g_down, row_down, col_down)
    return (token_grad, update_gate, update_up, update_down, row_gate_new, col_gate_new, row_up_new, col_up_new, row_down_new, col_down_new)
```

```python
import functools

import jax
import jax.numpy as jnp
from jax import lax
from jax.experimental import pallas as pl
from jax.experimental.pallas import tpu as pltpu
from jax.sharding import PartitionSpec as P

epsilon_one = 1e-30
decay_rate = 0.8
BF = jnp.bfloat16
F32 = jnp.float32
MIB = 1024 * 1024
EARLY = 16
FIRST = (((2, 0), (2, 1)), ((1, 1), (3, 0)))
SECOND = (((1, 0), (3, 1)), ((0, 0), (0, 1)))


def dp_shift(dz=0, dx=0, dc=0):
    pairs = []
    for z in range(4):
        for x in range(2):
            for c in range(2):
                to = ((z + dz) % 4) * 4 + (x ^ dx) * 2 + (c ^ dc)
                pairs.append((z * 4 + x * 2 + c, to))
    return pairs


def mp_shift(dy=0, dx=0):
    return [(y * 2 + x, ((y + dy) % 4) * 2 + (x ^ dx)) for y in range(4) for x in range(2)]


def contract(a, b, dim_a, dim_b):
    return lax.dot_general(a, b, (((dim_a,), (dim_b,)), ((), ())), preferred_element_type=F32)


def local_kernel(name, kernel, scalars, arrays, outs, flops, after=(), limit=6):
    vmem = pl.BlockSpec(memory_space=pltpu.VMEM)
    count, late = len(arrays), len(after)

    def run(*refs):
        first = 0 if scalars is None else 1
        kernel(*refs[: first + count], *refs[first + count + late :])

    specs = [] if scalars is None else [pl.BlockSpec(memory_space=pltpu.SMEM)]
    operands = [] if scalars is None else [scalars]
    return pl.pallas_call(
        run,
        in_specs=specs + [vmem] * count + [pl.BlockSpec(memory_space=pl.ANY)] * late,
        out_specs=[vmem] * len(outs),
        out_shape=outs,
        compiler_params=pltpu.CompilerParams(vmem_limit_bytes=limit * MIB),
        cost_estimate=pl.CostEstimate(flops=flops // EARLY, bytes_accessed=1024, transcendentals=0),
        name=name,
    )(
        *operands,
        *[pltpu.with_memory_space_constraint(a, pltpu.VMEM) for a in arrays],
        *after,
    )


def near(shape, dtype):
    return pltpu.VMEM(shape, dtype)


def gate_kernel(tok_in, wg_in, gate, tok, wg, tok_sem, wg_sem):
    rows = [pl.ds(m * 256, 256) for m in range(3)]
    cols = [pl.ds(n * 256, 256) for n in range(4)]
    tok_copy = [pltpu.make_async_copy(tok_in.at[r, :], tok.at[r, :], tok_sem.at[m])
                for m, r in enumerate(rows)]
    wg_copy = [pltpu.make_async_copy(wg_in.at[:, c], wg.at[:, c], wg_sem.at[n])
               for n, c in enumerate(cols)]
    for copy in (tok_copy[0], wg_copy[0], tok_copy[1], tok_copy[2], *wg_copy[1:]):
        copy.start()
    for n, c in enumerate(cols):
        wg_copy[n].wait()
        for m, r in enumerate(rows):
            if n == 0:
                tok_copy[m].wait()
            gate[r, c] = contract(tok[r, :], wg[:, c], 1, 0)


def gate_pre(tokens, w_gate):
    vmem, hbm = pl.BlockSpec(memory_space=pltpu.VMEM), pl.BlockSpec(memory_space=pltpu.HBM)
    rows, width = tokens.shape
    units = w_gate.shape[1]
    return pl.pallas_call(
        gate_kernel,
        in_specs=[hbm, hbm],
        out_specs=[vmem] * 3,
        out_shape=[near((rows, units), F32), near(tokens.shape, BF), near(w_gate.shape, BF)],
        scratch_shapes=[pltpu.SemaphoreType.DMA((3,)), pltpu.SemaphoreType.DMA((4,))],
        compiler_params=pltpu.CompilerParams(vmem_limit_bytes=4 * MIB),
        cost_estimate=pl.CostEstimate(flops=1000000, bytes_accessed=1024, transcendentals=0),
        name="gate_pre",
    )(*[pltpu.with_memory_space_constraint(a, pltpu.HBM) for a in (tokens, w_gate)])


def up_kernel(idx, tok, wu, gate, act_out, slope_out, h_own, h_send):
    z, xh, core = idx[0], idx[1], idx[2]
    for r in range(4):
        cols = pl.ds(pl.multiple_of(lax.rem(z + r, 4) * 256, 256), 256)
        pre = gate[:, cols]
        up = contract(tok[...], wu[:, cols], 1, 0)
        sig = 1.0 / (1.0 + jnp.exp(-pre))
        act = pre * sig
        act_out[:, cols] = act
        slope_out[:, cols] = up * (sig * (1.0 + pre * (1.0 - sig)))
        hid = (act * up).astype(BF).T
        piece = [hid[k * 64 : (k + 1) * 64, :] for k in range(4)]
        own = [jnp.where(core == 0, piece[2 * a], piece[2 * a + 1]) for a in range(2)]
        send = [jnp.where(core == 0, piece[2 * a + 1], piece[2 * a]) for a in range(2)]
        rows = pl.ds(r * 64, 64)
        for ref, pair in ((h_own, own), (h_send, send)):
            ref[0, rows, :] = jnp.where(xh == 0, pair[1], pair[0])
            ref[1, rows, :] = jnp.where(xh == 0, pair[0], pair[1])


def grad_kernel(cot, wd, act, slope, out):
    for j in range(4):
        cols = pl.ds(j * 256, 256)
        grad = contract(cot[...], wd[cols, :], 1, 1)
        out[0, :, cols] = (grad * slope[:, cols]).astype(BF)
        out[1, :, cols] = (grad * act[:, cols]).astype(BF)


def down_kernel(side, scale, h_own, h_peer, cot, cot_peer, out):
    for j in range(4):
        cols = pl.ds(j * 512, 512)
        term = contract(h_own[side], cot[:, cols], 1, 0)
        term = term + contract(h_peer[side], cot_peer[:, cols], 1, 0)
        out[:, cols] = (term * scale).astype(BF)


def weight_kernel(plan, scale, idx, tok, tok_peer, grad, grad_peer, one, two):
    z, xh, core = idx[0], idx[1], idx[2]

    def block(ref, r, side):
        x = xh if side == 1 else 1 - xh
        at = ((lax.rem(z + r, 4) * 2 + x) * 2 + core) * 128
        return ref[:, pl.ds(pl.multiple_of(at, 128), 128)]

    for k in range(2):
        mine, theirs = (
            jnp.concatenate([block(ref, *plan[k][0]), block(ref, *plan[k][1])], axis=1)
            for ref in (tok, tok_peer)
        )
        for j in range(4):
            cols, to = pl.ds((j % 2) * 512, 512), pl.ds(j * 512, 512)
            term = contract(mine, grad[j // 2, :, cols], 0, 0)
            term = (term + contract(theirs, grad_peer[j // 2, :, cols], 0, 0)) * scale
            one[k, :, to] = term[:128, :].astype(BF)
            two[k, :, to] = term[128:, :].astype(BF)


def token_kernel(plan, idx, grad, wg, wu, one, two):
    y, xl = idx[3], idx[4]
    for k in range(2):
        for out, (r, side) in zip((one, two), plan[k]):
            x = xl if side == 1 else 1 - xl
            at = (lax.rem(y + r, 4) * 2 + x) * 256
            rows = pl.ds(pl.multiple_of(at, 256), 256)
            term = contract(grad[0], wg[rows, :], 1, 1) + contract(grad[1], wu[rows, :], 1, 1)
            out[k] = term.astype(BF)


def mix_kernel(own, got, right, left, mid, keep):
    for r, rows in ((2, 0), (1, 64), (3, 128), (0, 192)):
        at = pl.ds(((r) % 4) * 64, 64)
        for side in range(2):
            cols = pl.ds(side * 1024, 1024)
            total = (own[at, cols].astype(F32) + got[at, cols].astype(F32)).astype(BF)
            for place, first, second in ((right, (2, 0), (1, 1)), (left, (2, 1), (3, 0)),
                                         (mid, (1, 0), (3, 1)), (keep, (0, 0), (0, 1))):
                if (r, side) == first:
                    place[0] = total
                if (r, side) == second:
                    place[1] = total


def add(*terms):
    total = terms[0].astype(F32)
    for term in terms[1:]:
        total = total + term.astype(F32)
    return total


def moment_step(old_value, column_total, count):
    return decay_rate * old_value + (1.0 - decay_rate) * (column_total / count + epsilon_one)


def row_totals(values):
    folded = values[:, :128]
    for k in range(1, values.shape[1] // 128):
        folded = folded + values[:, k * 128 : (k + 1) * 128]
    return jnp.sum(folded.T, axis=0, keepdims=True)


def down_rows(row):
    return jnp.broadcast_to(row, (128, row.shape[1])).T


def rows_kernel(keep, near_one, end, got, g_gate, g_up, pay):
    units = g_gate.shape[1]
    sums = []
    for k, out in enumerate((g_gate, g_up)):
        cols = pl.ds(k * units, units)
        g = add(keep[1, :, cols], near_one[1, :, cols], end[:, cols], got[:, cols])
        out[...] = g
        sums.append(row_totals(g * g))
    block = jnp.concatenate(sums + [jnp.zeros((6, 128), F32)], axis=0)
    for k in range(pay.shape[0]):
        pay[k] = block


def columns_kernel(
    counts, g_gate, g_up, keep, left, right, end_a, end_b, rows, row_gate, row_up, row_down,
    g_down, gate_new, up_new, down_new, pay, gate_out, up_out, down_out, work,
):
    all_units, width = counts
    half = end_a.shape[1]
    g_down[:, :half] = add(keep[0], left[1], end_a[...])
    g_down[:, half:] = add(keep[1], right[1], end_b[...])
    total = rows[0]
    for k in range(1, rows.shape[0]):
        total = total + rows[k]
    gate_new[...] = moment_step(row_gate[...], total[0:1, :], all_units)
    up_new[...] = moment_step(row_up[...], total[1:2, :], all_units)
    down = g_down[...]
    down_new[...] = moment_step(row_down[...], row_totals(down * down), width)
    gate_out[...] = gate_new[...]
    up_out[...] = up_new[...]
    down_out[...] = down_new[...]
    at = 0
    for g, new in ((g_gate, gate_new), (g_up, up_new), (g_down, down_new)):
        blocks = g.shape[1] // 128
        scale = 1.0 / down_rows(new[...])
        for k in range(blocks):
            value = g[:, k * 128 : (k + 1) * 128]
            square = value * value
            work[pl.ds(at + k, 1), :] = jnp.sum(square, axis=0, keepdims=True)
            work[pl.ds(at + blocks + k, 1), :] = jnp.sum(square * scale, axis=0, keepdims=True)
        at += 2 * blocks
    for k, new in enumerate((gate_new, up_new, down_new)):
        work[pl.ds(at + k, 1), :] = jnp.broadcast_to(
            jnp.sum(new[...], axis=1, keepdims=True), (1, 128)
        )
    work[pl.ds(at + 3, 5), :] = jnp.zeros((5, 128), F32)
    for k in range(pay.shape[0]):
        pay[k] = work[...]


def spread(value):
    return jnp.broadcast_to(
        jnp.sum(jnp.sum(value, axis=0, keepdims=True), axis=1, keepdims=True), (1, 128)
    )


def partial_kernel(width, got, col_gate, col_up, gate_new, up_new, sums, pay, gate_out, up_out):
    total = got[0]
    for k in range(1, got.shape[0]):
        total = total + got[k]
    gate = moment_step(col_gate[...], total[0:8], width)
    up = moment_step(col_up[...], total[16:24], width)
    gate_new[...] = gate
    up_new[...] = up
    gate_out[...] = gate
    up_out[...] = up
    sums[...] = total[64:72]
    for k in range(pay.shape[0]):
        pay[k, 0:32, :] = total[32:64]
        pay[k, 32:40, :] = jnp.concatenate(
            [
                spread(total[8:16] / gate),
                spread(total[24:32] / up),
                total[66:67],
                jnp.zeros((5, 128), F32),
            ],
            axis=0,
        )


def update_kernel(
    counts, got, sums, col_down, g_gate, g_up, g_down, row_gate, row_up, row_down, col_gate, col_up,
    gate_out, up_out, down_out, down_new,
):
    all_units, width = counts
    total = got[0]
    for k in range(1, got.shape[0]):
        total = total + got[k]
    down = moment_step(col_down[...], total[0:16], all_units)
    down_new[...] = down
    entries = float(width * all_units)
    work = (
        (gate_out, g_gate, row_gate, col_gate[...], sums[0:1, :] / width, total[32:33]),
        (up_out, g_up, row_up, col_up[...], sums[1:2, :] / width, total[33:34]),
        (down_out, g_down, row_down, down, total[34:35] / all_units, spread(total[16:32] / down)),
    )
    for out, g, row, col, mean, squares in work:
        factor = jnp.sqrt(mean) / jnp.maximum(1.0, jnp.sqrt(mean * squares / entries))
        by_row = lax.rsqrt(down_rows(row[...]))
        by_col = lax.rsqrt(col) * factor
        for k in range(col.shape[0]):
            cols = pl.ds(k * 128, 128)
            out[:, cols] = g[:, cols] * by_row * by_col[k : k + 1, :]


def body(
    tokens, cotangent, w_gate, w_up, w_down, row_gate, col_gate, row_up, col_up, row_down, col_down
):
    rows, width = tokens.shape
    units = w_gate.shape[1]
    all_units = units * 8
    scale = float(rows * 16) ** (-0.5)
    dp, mp = lax.axis_index("dp"), lax.axis_index("mp")
    idx = jnp.stack([dp // 4, (dp // 2) % 2, dp % 2, mp // 2, mp % 2]).astype(jnp.int32)
    swap = dp_shift(dc=1)
    forth, back, across = dp_shift(dz=1), dp_shift(dz=3), dp_shift(dx=1)
    y_forth, y_back, x_across = mp_shift(dy=1), mp_shift(dy=3), mp_shift(dx=1)
    one = 2 * rows * width * units

    tok_peer = lax.ppermute(tokens, "dp", swap)
    cot_peer = lax.ppermute(cotangent, "dp", swap)
    square = near((rows, units), F32)
    gate, tokens, w_gate = gate_pre(tokens, w_gate)
    hid = near((2, units // 4, rows), BF)
    act, slope, h_own, h_send = local_kernel(
        "up_pre", up_kernel, idx, [tokens, w_up, gate], [square, square, hid, hid], one
    )
    h_peer = lax.ppermute(h_send, "dp", swap)
    (grad,) = local_kernel(
        "hidden_grad", grad_kernel, None, [cotangent, w_down, act, slope],
        [near((2, rows, units), BF)], one,
        after=(tok_peer, cot_peer),
    )
    grad_peer = lax.ppermute(grad, "dp", swap)

    def down_part(side, after):
        return local_kernel(
            "down", functools.partial(down_kernel, side, scale), None,
            [h_own, h_peer, cotangent, cot_peer], [near((units // 4, width), BF)], one // 2,
            after=after,
        )[0]

    def weight_part(plan, after):
        out = near((2, width // 16, 2 * units), BF)
        return local_kernel(
            "weight", functools.partial(weight_kernel, plan, scale), idx,
            [tokens, tok_peer, grad, grad_peer], [out, out], one, after=after,
        )

    def token_part(plan, after):
        out = near((2, rows, width // 8), BF)
        return local_kernel(
            "token_grad", functools.partial(token_kernel, plan), idx, [grad, w_gate, w_up],
            [out, out], one, after=after,
        )

    tok_r, tok_l = token_part(FIRST, ())
    pair_r, pair_l = weight_part(FIRST, (tok_r,))
    away = down_part(0, (pair_r,))
    pair_a, pair_b = weight_part(SECOND, (away,))
    tok_a, tok_b = token_part(SECOND, (pair_a,))
    own = down_part(1, (tok_a,))

    def ring_first(axis, pairs, right, left, mid_a, mid_b):
        from_left = lax.ppermute(right, axis, pairs[0])
        from_right = lax.ppermute(left, axis, pairs[1])
        onward = add(mid_a, from_left[0]).astype(BF)
        backward = add(mid_b, from_right[0]).astype(BF)
        return onward, backward, from_left, from_right

    def ring_second(axis, pairs, onward, backward):
        return lax.ppermute(onward, axis, pairs[0]), lax.ppermute(backward, axis, pairs[1])

    ring, y_ring = (forth, back), (y_forth, y_back)
    pair_mid = ring_first("dp", ring, pair_r, pair_l, pair_a[0], pair_b[0])
    pair_end = ring_second("dp", ring, *pair_mid[:2])
    part = near((2, units // 16, width // 2), BF)
    down_r, down_l, down_m, down_k = local_kernel(
        "down_mix", mix_kernel, None, [own, lax.ppermute(away, "dp", across)], [part] * 4, 1000
    )
    down_mid = ring_first("dp", ring, down_r, down_l, down_m[0], down_m[1])
    down_end = ring_second("dp", ring, *down_mid[:2])
    tok_mid = ring_first("mp", y_ring, tok_r, tok_l, tok_a[0], tok_b[0])
    tok_end = ring_second("mp", y_ring, *tok_mid[:2])

    def cross(keep, mid, end, axis, pairs):
        return lax.ppermute(add(keep[1], mid[3][1], end[0]).astype(BF), axis, pairs)

    pair_got = cross(pair_a, pair_mid, pair_end, "dp", across)
    tok_got = cross(tok_a, tok_mid, tok_end, "mp", x_across)
    token_grad = add(tok_b[1], tok_mid[2][1], tok_end[1], tok_got).astype(BF)

    shard = near((width // 16, units), F32)
    g_gate, g_up, pay = local_kernel(
        "row_sums", rows_kernel, None,
        [pair_b, pair_mid[2], pair_end[1], pair_got],
        [shard, shard, near((8, 8, 128), F32)], 1000, after=(token_grad,), limit=4,
    )
    row_got = lax.all_to_all(pay, "mp", 0, 0, tiled=True)

    counts = (all_units, width)
    line = near((1, width // 16), F32)
    short = near((1, units // 16), F32)
    line_out = jax.ShapeDtypeStruct((1, width // 16), F32)
    short_out = jax.ShapeDtypeStruct((1, units // 16), F32)
    g_down, row_gate_new, row_up_new, row_down_new, pay, *rows_out, _ = local_kernel(
        "column_sums", functools.partial(columns_kernel, counts), None,
        [
            g_gate, g_up, down_k, down_mid[3], down_mid[2], *down_end, row_got,
            row_gate.reshape(1, -1), row_up.reshape(1, -1), row_down.reshape(1, -1),
        ],
        [near((units // 16, width), F32), line, line, short, near((16, 72, 128), F32),
         line_out, line_out, short_out, near((72, 128), F32)],
        1000, limit=4,
    )
    col_got = lax.all_to_all(pay, "dp", 0, 0, tiled=True)

    lines = near((units // 128, 128), F32)
    lines_out = jax.ShapeDtypeStruct((units // 128, 128), F32)
    col_gate_new, col_up_new, sums, pay, *cols_out = local_kernel(
        "partial_sums", functools.partial(partial_kernel, width), None,
        [col_got, col_gate.reshape(-1, 128), col_up.reshape(-1, 128)],
        [lines, lines, near((8, 128), F32), near((8, 40, 128), F32), lines_out, lines_out], 1000, limit=4,
    )
    last = lax.all_to_all(pay, "mp", 0, 0, tiled=True)
    update_gate, update_up, update_down, col_down_new = local_kernel(
        "updates", functools.partial(update_kernel, counts), None,
        [
            last, sums, col_down.reshape(-1, 128), g_gate, g_up, g_down,
            row_gate_new, row_up_new, row_down_new, col_gate_new, col_up_new,
        ],
        [
            jax.ShapeDtypeStruct((width // 16, units), F32),
            jax.ShapeDtypeStruct((width // 16, units), F32),
            jax.ShapeDtypeStruct((units // 16, width), F32),
            jax.ShapeDtypeStruct((width // 128, 128), F32),
        ],
        1000, limit=8,
    )
    return (
        token_grad,
        update_gate,
        update_up,
        update_down,
        rows_out[0].reshape(-1),
        cols_out[0].reshape(-1),
        rows_out[1].reshape(-1),
        cols_out[1].reshape(-1),
        rows_out[2].reshape(-1),
        col_down_new.reshape(-1),
    )


def solution(mesh):
    in_specs = (
        P("dp", None),
        P("dp", None),
        P(None, "mp"),
        P(None, "mp"),
        P("mp", None),
        P("dp"),
        P("mp"),
        P("dp"),
        P("mp"),
        P(("mp", "dp")),
        P(),
    )
    out_specs = (
        P("dp", "mp"),
        P("dp", "mp"),
        P("dp", "mp"),
        P(("mp", "dp"), None),
        P("dp"),
        P("mp"),
        P("dp"),
        P("mp"),
        P(("mp", "dp")),
        P(),
    )
    return jax.shard_map(body, mesh=mesh, in_specs=in_specs, out_specs=out_specs, check_vma=False)
```

```python
import functools

import jax
import jax.numpy as jnp
from jax import lax
from jax.experimental import pallas as pl
from jax.experimental.pallas import tpu as pltpu
from jax.sharding import PartitionSpec as P

epsilon_one = 1e-30
decay_rate = 0.8
BF = jnp.bfloat16
F32 = jnp.float32
MIB = 1024 * 1024
EARLY = 16
FIRST = (((2, 0), (2, 1)), ((1, 1), (3, 0)))
SECOND = (((1, 0), (3, 1)), ((0, 0), (0, 1)))


def dp_shift(dz=0, dx=0, dc=0):
    pairs = []
    for z in range(4):
        for x in range(2):
            for c in range(2):
                to = ((z + dz) % 4) * 4 + (x ^ dx) * 2 + (c ^ dc)
                pairs.append((z * 4 + x * 2 + c, to))
    return pairs


def dp_pairs(flip):
    return [(k, (((k // 4) ^ flip) * 4) + k % 4) for k in range(16)]


def mp_shift(dy=0, dx=0):
    return [(y * 2 + x, ((y + dy) % 4) * 2 + (x ^ dx)) for y in range(4) for x in range(2)]


def contract(a, b, dim_a, dim_b):
    return lax.dot_general(a, b, (((dim_a,), (dim_b,)), ((), ())), preferred_element_type=F32)


def local_kernel(name, kernel, scalars, arrays, outs, flops, after=(), limit=6):
    vmem = pl.BlockSpec(memory_space=pltpu.VMEM)
    count, late = len(arrays), len(after)

    def run(*refs):
        first = 0 if scalars is None else 1
        kernel(*refs[: first + count], *refs[first + count + late :])

    specs = [] if scalars is None else [pl.BlockSpec(memory_space=pltpu.SMEM)]
    operands = [] if scalars is None else [scalars]
    return pl.pallas_call(
        run,
        in_specs=specs + [vmem] * count + [pl.BlockSpec(memory_space=pl.ANY)] * late,
        out_specs=[vmem] * len(outs),
        out_shape=outs,
        compiler_params=pltpu.CompilerParams(vmem_limit_bytes=limit * MIB),
        cost_estimate=pl.CostEstimate(flops=flops // EARLY, bytes_accessed=1024, transcendentals=0),
        name=name,
    )(
        *operands,
        *[pltpu.with_memory_space_constraint(a, pltpu.VMEM) for a in arrays],
        *after,
    )


def near(shape, dtype):
    return pltpu.VMEM(shape, dtype)


def gate_kernel(idx, tok_in, wg_in, gate, tok, wg, tok_sem, wg_sem):
    rows = [pl.ds(m * 256, 256) for m in range(3)]
    deep = [pl.ds(n * 256, 256) for n in range(8)]
    wg_copy = [pltpu.make_async_copy(wg_in.at[d, :], wg.at[d, :], wg_sem.at[n])
               for n, d in enumerate(deep)]
    tok_copy = [pltpu.make_async_copy(tok_in.at[r, :], tok.at[r, :], tok_sem.at[m])
                for m, r in enumerate(rows)]
    for copy in (tok_copy[0], *wg_copy, *tok_copy[1:]):
        copy.start()
    for copy in wg_copy:
        copy.wait()
    for m, r in enumerate(rows):
        tok_copy[m].wait()
        for n in range(2):
            c = pl.ds(n * 512, 512)
            gate[r, c] = contract(tok[r, :], wg[:, c], 1, 0)


def gate_pre(idx, tokens, w_gate):
    vmem, hbm = pl.BlockSpec(memory_space=pltpu.VMEM), pl.BlockSpec(memory_space=pltpu.HBM)
    rows, width = tokens.shape
    units = w_gate.shape[1]
    return pl.pallas_call(
        gate_kernel,
        in_specs=[pl.BlockSpec(memory_space=pltpu.SMEM), hbm, hbm],
        out_specs=[vmem] * 3,
        out_shape=[near((rows, units), F32), near(tokens.shape, BF), near(w_gate.shape, BF)],
        scratch_shapes=[pltpu.SemaphoreType.DMA((3,)), pltpu.SemaphoreType.DMA((8,))],
        compiler_params=pltpu.CompilerParams(vmem_limit_bytes=4 * MIB),
        cost_estimate=pl.CostEstimate(flops=1000000, bytes_accessed=1024, transcendentals=0),
        name="gate_pre",
    )(idx, *[pltpu.with_memory_space_constraint(a, pltpu.HBM) for a in (tokens, w_gate)])


def up_kernel(idx, tok, wu, gate, act_out, slope_out, h_own, h_send):
    z, xh, core = idx[0], idx[1], idx[2]
    for r, far in enumerate((2, 1, 3, 0)):
        cols = pl.ds(pl.multiple_of(lax.bitwise_xor(z, far) * 256, 256), 256)
        pre = gate[:, cols]
        up = contract(tok[...], wu[:, cols], 1, 0)
        sig = 1.0 / (1.0 + jnp.exp(-pre))
        act = pre * sig
        act_out[:, cols] = act
        slope_out[:, cols] = up * (sig * (1.0 + pre * (1.0 - sig)))
        hid = (act * up).astype(BF).T
        piece = [hid[k * 64 : (k + 1) * 64, :] for k in range(4)]
        own = [jnp.where(core == 0, piece[2 * a], piece[2 * a + 1]) for a in range(2)]
        send = [jnp.where(core == 0, piece[2 * a + 1], piece[2 * a]) for a in range(2)]
        rows = pl.ds(r * 64, 64)
        for ref, pair in ((h_own, own), (h_send, send)):
            ref[0, rows, :] = jnp.where(xh == 0, pair[1], pair[0])
            ref[1, rows, :] = jnp.where(xh == 0, pair[0], pair[1])


def grad_kernel(cot, wd, act, slope, out):
    for j in range(4):
        cols = pl.ds(j * 256, 256)
        grad = contract(cot[...], wd[cols, :], 1, 1)
        out[0, :, cols] = (grad * slope[:, cols]).astype(BF)
        out[1, :, cols] = (grad * act[:, cols]).astype(BF)


def down_kernel(side, scale, h_own, h_peer, cot, cot_peer, out):
    for j in range(4):
        cols = pl.ds(j * 512, 512)
        term = contract(h_own[side], cot[:, cols], 1, 0)
        term = term + contract(h_peer[side], cot_peer[:, cols], 1, 0)
        out[:, cols] = (term * scale).astype(BF)


def weight_kernel(plan, scale, idx, tok, tok_peer, grad, grad_peer, one, two):
    z, xh, core = idx[0], idx[1], idx[2]

    def block(ref, r, side):
        x = xh if side == 1 else 1 - xh
        at = ((lax.rem(z + r, 4) * 2 + x) * 2 + core) * 128
        return ref[:, pl.ds(pl.multiple_of(at, 128), 128)]

    for k in range(2):
        mine, theirs = (
            jnp.concatenate([block(ref, *plan[k][0]), block(ref, *plan[k][1])], axis=1)
            for ref in (tok, tok_peer)
        )
        for j in range(4):
            cols, to = pl.ds((j % 2) * 512, 512), pl.ds(j * 512, 512)
            term = contract(mine, grad[j // 2, :, cols], 0, 0)
            term = (term + contract(theirs, grad_peer[j // 2, :, cols], 0, 0)) * scale
            one[k, :, to] = term[:128, :].astype(BF)
            two[k, :, to] = term[128:, :].astype(BF)


def token_kernel(plan, idx, grad, wg, wu, one, two):
    y, xl = idx[3], idx[4]
    for k in range(2):
        for out, (r, side) in zip((one, two), plan[k]):
            x = xl if side == 1 else 1 - xl
            at = (lax.rem(y + r, 4) * 2 + x) * 256
            rows = pl.ds(pl.multiple_of(at, 256), 256)
            term = contract(grad[0], wg[rows, :], 1, 1) + contract(grad[1], wu[rows, :], 1, 1)
            out[k] = term.astype(BF)


def mix_kernel(own, got, send, keep):
    half = send.shape[0]
    send[...] = add(own[:half, :], got[:half, :]).astype(BF)
    keep[...] = add(own[half:, :], got[half:, :]).astype(BF)


def add(*terms):
    total = terms[0].astype(F32)
    for term in terms[1:]:
        total = total + term.astype(F32)
    return total


def middle_kernel(one, two, from_left, from_right, onward, backward):
    onward[...] = add(one[0], from_left[0]).astype(BF)
    backward[...] = add(two[0], from_right[0]).astype(BF)


def crossing_kernel(keep, got, end, out):
    out[...] = add(keep[1], got[1], end[...]).astype(BF)


def down_middle_kernel(keep, got, out):
    size = out.shape[0]
    out[...] = add(keep[:size, :], got[:size, :]).astype(BF)


def token_end_kernel(keep, got, end, last, out, ended):
    ended[...] = jnp.zeros_like(ended)
    out[...] = add(keep[1], got[1], end[...], last[...]).astype(BF)


def moment_step(old_value, column_total, count):
    return decay_rate * old_value + (1.0 - decay_rate) * (column_total / count + epsilon_one)


def row_totals(values):
    folded = values[:, :128]
    for k in range(1, values.shape[1] // 128):
        folded = folded + values[:, k * 128 : (k + 1) * 128]
    return jnp.sum(folded.T, axis=0, keepdims=True)


def down_rows(row):
    return jnp.broadcast_to(row, (128, row.shape[1])).T


def rows_kernel(keep, near_one, end, got, g_gate, g_up, pay):
    units = g_gate.shape[1]
    sums = []
    for k, out in enumerate((g_gate, g_up)):
        cols = pl.ds(k * units, units)
        g = add(keep[1, :, cols], near_one[1, :, cols], end[:, cols], got[:, cols])
        out[...] = g
        sums.append(row_totals(g * g))
    block = jnp.concatenate(sums + [jnp.zeros((6, 128), F32)], axis=0)
    for k in range(pay.shape[0]):
        pay[k] = block


def columns_kernel(
    counts, g_gate, g_up, keep, near_one, end, rows, row_gate, row_up, row_down,
    g_down, gate_new, up_new, down_new, pay, gate_out, up_out, down_out, work,
):
    all_units, width = counts
    size = g_down.shape[0]
    g_down[...] = add(keep[size:, :], near_one[size:, :], end[...])
    total = rows[0]
    for k in range(1, rows.shape[0]):
        total = total + rows[k]
    gate_new[...] = moment_step(row_gate[...], total[0:1, :], all_units)
    up_new[...] = moment_step(row_up[...], total[1:2, :], all_units)
    down = g_down[...]
    down_new[...] = moment_step(row_down[...], row_totals(down * down), width)
    gate_out[...] = gate_new[...]
    up_out[...] = up_new[...]
    down_out[...] = down_new[...]
    at = 0
    for g, new in ((g_gate, gate_new), (g_up, up_new), (g_down, down_new)):
        blocks = g.shape[1] // 128
        scale = 1.0 / down_rows(new[...])
        for k in range(blocks):
            value = g[:, k * 128 : (k + 1) * 128]
            square = value * value
            work[pl.ds(at + k, 1), :] = jnp.sum(square, axis=0, keepdims=True)
            work[pl.ds(at + blocks + k, 1), :] = jnp.sum(square * scale, axis=0, keepdims=True)
        at += 2 * blocks
    sums = jnp.concatenate(
        [
            jnp.broadcast_to(jnp.sum(new[...], axis=1, keepdims=True), (1, 128))
            for new in (gate_new, up_new, down_new)
        ]
        + [jnp.zeros((5, 128), F32)],
        axis=0,
    )
    high = sums.astype(BF).astype(F32)
    work[64:72, :] = high
    work[72:80, :] = sums - high
    block = work[...].astype(BF)
    for k in range(pay.shape[0]):
        pay[k] = block


def spread(value):
    return jnp.broadcast_to(
        jnp.sum(jnp.sum(value, axis=0, keepdims=True), axis=1, keepdims=True), (1, 128)
    )


def partial_kernel(width, got, col_gate, col_up, gate_new, up_new, sums, pay, gate_out, up_out):
    total = add(*[got[k] for k in range(got.shape[0])])
    row_sums = total[64:72] + total[72:80]
    gate = moment_step(col_gate[...], total[0:8], width)
    up = moment_step(col_up[...], total[16:24], width)
    gate_new[...] = gate
    up_new[...] = up
    gate_out[...] = gate
    up_out[...] = up
    sums[...] = row_sums
    for k in range(pay.shape[0]):
        pay[k, 0:32, :] = total[32:64]
        pay[k, 32:40, :] = jnp.concatenate(
            [
                spread(total[8:16] / gate),
                spread(total[24:32] / up),
                row_sums[2:3],
                jnp.zeros((5, 128), F32),
            ],
            axis=0,
        )


def update_kernel(
    counts, got, sums, col_down, g_gate, g_up, g_down, row_gate, row_up, row_down, col_gate, col_up,
    gate_out, up_out, down_out, down_new,
):
    all_units, width = counts
    total = got[0]
    for k in range(1, got.shape[0]):
        total = total + got[k]
    down = moment_step(col_down[...], total[0:16], all_units)
    down_new[...] = down
    entries = float(width * all_units)
    work = (
        (gate_out, g_gate, row_gate, col_gate[...], sums[0:1, :] / width, total[32:33]),
        (up_out, g_up, row_up, col_up[...], sums[1:2, :] / width, total[33:34]),
        (down_out, g_down, row_down, down, total[34:35] / all_units, spread(total[16:32] / down)),
    )
    for out, g, row, col, mean, squares in work:
        factor = jnp.sqrt(mean) / jnp.maximum(1.0, jnp.sqrt(mean * squares / entries))
        by_row = lax.rsqrt(down_rows(row[...]))
        by_col = lax.rsqrt(col) * factor
        for k in range(col.shape[0]):
            cols = pl.ds(k * 128, 128)
            out[:, cols] = g[:, cols] * by_row * by_col[k : k + 1, :]


def body(
    tokens, cotangent, w_gate, w_up, w_down, row_gate, col_gate, row_up, col_up, row_down, col_down
):
    rows, width = tokens.shape
    units = w_gate.shape[1]
    all_units = units * 8
    scale = float(rows * 16) ** (-0.5)
    dp, mp = lax.axis_index("dp"), lax.axis_index("mp")
    idx = jnp.stack([dp // 4, (dp // 2) % 2, dp % 2, mp // 2, mp % 2]).astype(jnp.int32)
    swap = dp_shift(dc=1)
    forth, back, across = dp_shift(dz=1), dp_shift(dz=3), dp_shift(dx=1)
    y_forth, y_back, x_across = mp_shift(dy=1), mp_shift(dy=3), mp_shift(dx=1)
    one = 2 * rows * width * units

    cot_peer = lax.ppermute(cotangent, "dp", swap)
    square = near((rows, units), F32)
    gate, tokens, w_gate = gate_pre(idx, tokens, w_gate)
    tok_peer = lax.ppermute(tokens, "dp", swap)
    hid = near((2, units // 4, rows), BF)
    act, slope, h_own, h_send = local_kernel(
        "up_pre", up_kernel, idx, [tokens, w_up, gate], [square, square, hid, hid], one
    )
    h_peer = lax.ppermute(h_send, "dp", swap)
    (grad,) = local_kernel(
        "hidden_grad", grad_kernel, None, [cotangent, w_down, act, slope],
        [near((2, rows, units), BF)], one,
        after=(tok_peer, cot_peer),
    )
    grad_peer = lax.ppermute(grad, "dp", swap)

    def down_part(side, after):
        return local_kernel(
            "down", functools.partial(down_kernel, side, scale), None,
            [h_own, h_peer, cotangent, cot_peer], [near((units // 4, width), BF)], one // 2,
            after=after,
        )[0]

    def weight_part(plan, after):
        out = near((2, width // 16, 2 * units), BF)
        return local_kernel(
            "weight", functools.partial(weight_kernel, plan, scale), idx,
            [tokens, tok_peer, grad, grad_peer], [out, out], one, after=after,
        )

    def token_part(plan, after):
        out = near((2, rows, width // 8), BF)
        return local_kernel(
            "token_grad", functools.partial(token_kernel, plan), idx, [grad, w_gate, w_up],
            [out, out], one, after=after,
        )

    tok_r, tok_l = token_part(FIRST, ())
    pair_r, pair_l = weight_part(FIRST, (tok_r,))
    away = down_part(0, (pair_r,))
    pair_a, pair_b = weight_part(SECOND, (away,))
    tok_a, tok_b = token_part(SECOND, (pair_a,))
    own = down_part(1, (tok_a,))

    def middle(parts, got, after):
        out = near(parts[0].shape[1:], BF)
        return local_kernel("middle", middle_kernel, None, [*parts, *got], [out, out], 1000,
                            after=after)

    def crossing(keep, got, end, after):
        out = near(end.shape, BF)
        return local_kernel("crossing", crossing_kernel, None, [keep, got, end], [out], 1000,
                            after=after)[0]

    tok_got = lax.ppermute(tok_r, "mp", y_forth), lax.ppermute(tok_l, "mp", y_back)
    tok_mid = middle((tok_a, tok_b), tok_got, (own,))
    tok_end = lax.ppermute(tok_mid[0], "mp", y_forth), lax.ppermute(tok_mid[1], "mp", y_back)
    pair_got = lax.ppermute(pair_r, "dp", forth), lax.ppermute(pair_l, "dp", back)
    pair_mid = middle((pair_a, pair_b), pair_got, (tok_mid[0],))
    pair_end = lax.ppermute(pair_mid[0], "dp", forth), lax.ppermute(pair_mid[1], "dp", back)
    tok_away = crossing(tok_a, tok_got[1], tok_end[0], (pair_mid[0], tok_end[1]))
    tok_last = lax.ppermute(tok_away, "mp", x_across)
    part = near((units // 8, width), BF)
    down_away, down_keep = local_kernel(
        "down_mix", mix_kernel, None, [own, lax.ppermute(away, "dp", across)], [part] * 2, 1000,
        after=(tok_away,),
    )
    down_got = lax.ppermute(down_away, "dp", dp_pairs(1))
    pair_away = crossing(pair_a, pair_got[1], pair_end[0], (down_away, pair_end[1], tok_last))
    pair_last = lax.ppermute(pair_away, "dp", across)
    (down_mid,) = local_kernel(
        "down_middle", down_middle_kernel, None, [down_keep, down_got],
        [near((units // 16, width), BF)], 1000, after=(pair_away,),
    )
    down_end = lax.ppermute(down_mid, "dp", dp_pairs(3))
    token_grad, tok_ended = local_kernel(
        "token_end", token_end_kernel, None, [tok_b, tok_got[0], tok_end[1], tok_last],
        [jax.ShapeDtypeStruct((rows, width // 8), BF), near((8, 128), F32)], 1000,
        after=(down_mid,),
    )

    shard = near((width // 16, units), F32)
    g_gate, g_up, pay = local_kernel(
        "row_sums", rows_kernel, None,
        [pair_b, pair_got[0], pair_end[1], pair_last],
        [shard, shard, near((8, 8, 128), F32)], 1000, after=(tok_ended,), limit=4,
    )
    row_got = lax.all_to_all(pay, "mp", 0, 0, tiled=True)

    counts = (all_units, width)
    line = near((1, width // 16), F32)
    short = near((1, units // 16), F32)
    line_out = jax.ShapeDtypeStruct((1, width // 16), F32)
    short_out = jax.ShapeDtypeStruct((1, units // 16), F32)
    g_down, row_gate_new, row_up_new, row_down_new, pay, *rows_out, _ = local_kernel(
        "column_sums", functools.partial(columns_kernel, counts), None,
        [
            g_gate, g_up, down_keep, down_got, down_end, row_got,
            row_gate.reshape(1, -1), row_up.reshape(1, -1), row_down.reshape(1, -1),
        ],
        [near((units // 16, width), F32), line, line, short, near((16, 80, 128), BF),
         line_out, line_out, short_out, near((80, 128), F32)],
        1000, limit=4,
    )
    col_got = lax.all_to_all(pay, "dp", 0, 0, tiled=True)

    lines = near((units // 128, 128), F32)
    lines_out = jax.ShapeDtypeStruct((units // 128, 128), F32)
    col_gate_new, col_up_new, sums, pay, *cols_out = local_kernel(
        "partial_sums", functools.partial(partial_kernel, width), None,
        [col_got, col_gate.reshape(-1, 128), col_up.reshape(-1, 128)],
        [lines, lines, near((8, 128), F32), near((8, 40, 128), F32), lines_out, lines_out], 1000, limit=4,
    )
    last = lax.all_to_all(pay, "mp", 0, 0, tiled=True)
    update_gate, update_up, update_down, col_down_new = local_kernel(
        "updates", functools.partial(update_kernel, counts), None,
        [
            last, sums, col_down.reshape(-1, 128), g_gate, g_up, g_down,
            row_gate_new, row_up_new, row_down_new, col_gate_new, col_up_new,
        ],
        [
            jax.ShapeDtypeStruct((width // 16, units), F32),
            jax.ShapeDtypeStruct((width // 16, units), F32),
            jax.ShapeDtypeStruct((units // 16, width), F32),
            jax.ShapeDtypeStruct((width // 128, 128), F32),
        ],
        1000, limit=8,
    )
    return (
        token_grad,
        update_gate,
        update_up,
        update_down,
        rows_out[0].reshape(-1),
        cols_out[0].reshape(-1),
        rows_out[1].reshape(-1),
        cols_out[1].reshape(-1),
        rows_out[2].reshape(-1),
        col_down_new.reshape(-1),
    )


def solution(mesh):
    in_specs = (
        P("dp", None),
        P("dp", None),
        P(None, "mp"),
        P(None, "mp"),
        P("mp", None),
        P("dp"),
        P("mp"),
        P("dp"),
        P("mp"),
        P(("mp", "dp")),
        P(),
    )
    out_specs = (
        P("dp", "mp"),
        P("dp", "mp"),
        P("dp", "mp"),
        P(("mp", "dp"), None),
        P("dp"),
        P("mp"),
        P("dp"),
        P("mp"),
        P(("mp", "dp")),
        P(),
    )
    return jax.shard_map(body, mesh=mesh, in_specs=in_specs, out_specs=out_specs, check_vma=False)
```

```python
import functools

import jax
import jax.numpy as jnp
from jax import lax
from jax.experimental import pallas as pl
from jax.experimental.pallas import tpu as pltpu
from jax.sharding import PartitionSpec as P

epsilon_one = 1e-30
decay_rate = 0.8
BF = jnp.bfloat16
F32 = jnp.float32
MIB = 1024 * 1024
EARLY = 16
FIRST = (((2, 0), (2, 1)), ((1, 1), (3, 0)))
SECOND = (((1, 0), (3, 1)), ((0, 0), (0, 1)))


def dp_shift(dz=0, dx=0, dc=0):
    pairs = []
    for z in range(4):
        for x in range(2):
            for c in range(2):
                to = ((z + dz) % 4) * 4 + (x ^ dx) * 2 + (c ^ dc)
                pairs.append((z * 4 + x * 2 + c, to))
    return pairs


def dp_pairs(flip):
    return [(k, (((k // 4) ^ flip) * 4) + k % 4) for k in range(16)]


def mp_shift(dy=0, dx=0):
    return [(y * 2 + x, ((y + dy) % 4) * 2 + (x ^ dx)) for y in range(4) for x in range(2)]


def contract(a, b, dim_a, dim_b):
    return lax.dot_general(a, b, (((dim_a,), (dim_b,)), ((), ())), preferred_element_type=F32)


def local_kernel(name, kernel, scalars, arrays, outs, flops, after=(), limit=6):
    vmem = pl.BlockSpec(memory_space=pltpu.VMEM)
    count, late = len(arrays), len(after)

    def run(*refs):
        first = 0 if scalars is None else 1
        kernel(*refs[: first + count], *refs[first + count + late :])

    specs = [] if scalars is None else [pl.BlockSpec(memory_space=pltpu.SMEM)]
    operands = [] if scalars is None else [scalars]
    return pl.pallas_call(
        run,
        in_specs=specs + [vmem] * count + [pl.BlockSpec(memory_space=pl.ANY)] * late,
        out_specs=[vmem] * len(outs),
        out_shape=outs,
        compiler_params=pltpu.CompilerParams(vmem_limit_bytes=limit * MIB),
        cost_estimate=pl.CostEstimate(flops=flops // EARLY, bytes_accessed=1024, transcendentals=0),
        name=name,
    )(
        *operands,
        *[pltpu.with_memory_space_constraint(a, pltpu.VMEM) for a in arrays],
        *after,
    )


def near(shape, dtype):
    return pltpu.VMEM(shape, dtype)


def gate_kernel(idx, tok_in, wg_in, wu_in, gate, tok, wg, wu, tok_sem, wg_sem, wu_sem):
    rows = [pl.ds(m * 256, 256) for m in range(3)]
    deep = [pl.ds(n * 256, 256) for n in range(8)]
    wg_copy = [pltpu.make_async_copy(wg_in.at[d, :], wg.at[d, :], wg_sem.at[n])
               for n, d in enumerate(deep)]
    tok_copy = [pltpu.make_async_copy(tok_in.at[r, :], tok.at[r, :], tok_sem.at[m])
                for m, r in enumerate(rows)]
    wu_copy = pltpu.make_async_copy(wu_in, wu, wu_sem)
    for copy in (tok_copy[0], *wg_copy, *tok_copy[1:], wu_copy):
        copy.start()
    for copy in wg_copy:
        copy.wait()
    for m, r in enumerate(rows):
        tok_copy[m].wait()
        for n in range(2):
            c = pl.ds(n * 512, 512)
            gate[r, c] = contract(tok[r, :], wg[:, c], 1, 0)
    wu_copy.wait()


def gate_pre(idx, tokens, w_gate, w_up):
    vmem, hbm = pl.BlockSpec(memory_space=pltpu.VMEM), pl.BlockSpec(memory_space=pltpu.HBM)
    rows, width = tokens.shape
    units = w_gate.shape[1]
    return pl.pallas_call(
        gate_kernel,
        in_specs=[pl.BlockSpec(memory_space=pltpu.SMEM), hbm, hbm, hbm],
        out_specs=[vmem] * 4,
        out_shape=[near((rows, units), F32), near(tokens.shape, BF), near(w_gate.shape, BF),
                   near(w_up.shape, BF)],
        scratch_shapes=[pltpu.SemaphoreType.DMA((3,)), pltpu.SemaphoreType.DMA((8,)),
                        pltpu.SemaphoreType.DMA],
        compiler_params=pltpu.CompilerParams(vmem_limit_bytes=4 * MIB),
        cost_estimate=pl.CostEstimate(flops=1000000, bytes_accessed=1024, transcendentals=0),
        name="gate_pre",
    )(idx, *[pltpu.with_memory_space_constraint(a, pltpu.HBM) for a in (tokens, w_gate, w_up)])


def up_kernel(idx, tok, wu, gate, act_out, slope_out, h_own, h_send):
    z, xh, core = idx[0], idx[1], idx[2]
    for r, far in enumerate((2, 1, 3, 0)):
        cols = pl.ds(pl.multiple_of(lax.bitwise_xor(z, far) * 256, 256), 256)
        pre = gate[:, cols]
        up = contract(tok[...], wu[:, cols], 1, 0)
        sig = 1.0 / (1.0 + jnp.exp(-pre))
        act = pre * sig
        act_out[:, cols] = act
        slope_out[:, cols] = up * (sig * (1.0 + pre * (1.0 - sig)))
        hid = (act * up).astype(BF).T
        piece = [hid[k * 64 : (k + 1) * 64, :] for k in range(4)]
        own = [jnp.where(core == 0, piece[2 * a], piece[2 * a + 1]) for a in range(2)]
        send = [jnp.where(core == 0, piece[2 * a + 1], piece[2 * a]) for a in range(2)]
        rows = pl.ds(r * 64, 64)
        for ref, pair in ((h_own, own), (h_send, send)):
            ref[0, rows, :] = jnp.where(xh == 0, pair[1], pair[0])
            ref[1, rows, :] = jnp.where(xh == 0, pair[0], pair[1])


def grad_kernel(cot, wd, act, slope, out):
    for j in range(4):
        cols = pl.ds(j * 256, 256)
        grad = contract(cot[...], wd[cols, :], 1, 1)
        out[0, :, cols] = (grad * slope[:, cols]).astype(BF)
        out[1, :, cols] = (grad * act[:, cols]).astype(BF)


def down_kernel(side, scale, h_own, h_peer, cot, cot_peer, out):
    for j in range(4):
        cols = pl.ds(j * 512, 512)
        term = contract(h_own[side], cot[:, cols], 1, 0)
        term = term + contract(h_peer[side], cot_peer[:, cols], 1, 0)
        out[:, cols] = (term * scale).astype(BF)


def weight_kernel(plan, scale, idx, tok, tok_peer, grad, grad_peer, one, two):
    z, xh, core = idx[0], idx[1], idx[2]

    def block(ref, r, side):
        x = xh if side == 1 else 1 - xh
        at = ((lax.rem(z + r, 4) * 2 + x) * 2 + core) * 128
        return ref[:, pl.ds(pl.multiple_of(at, 128), 128)]

    for k in range(2):
        mine, theirs = (
            jnp.concatenate([block(ref, *plan[k][0]), block(ref, *plan[k][1])], axis=1)
            for ref in (tok, tok_peer)
        )
        for j in range(4):
            cols, to = pl.ds((j % 2) * 512, 512), pl.ds(j * 512, 512)
            term = contract(mine, grad[j // 2, :, cols], 0, 0)
            term = (term + contract(theirs, grad_peer[j // 2, :, cols], 0, 0)) * scale
            one[k, :, to] = term[:128, :].astype(BF)
            two[k, :, to] = term[128:, :].astype(BF)


def token_kernel(plan, idx, grad, wg, wu, one, two):
    y, xl = idx[3], idx[4]
    for k in range(2):
        for out, (r, side) in zip((one, two), plan[k]):
            x = xl if side == 1 else 1 - xl
            at = (lax.rem(y + r, 4) * 2 + x) * 256
            rows = pl.ds(pl.multiple_of(at, 256), 256)
            term = contract(grad[0], wg[rows, :], 1, 1) + contract(grad[1], wu[rows, :], 1, 1)
            out[k] = term.astype(BF)


def mix_kernel(own, got, send, keep):
    half = send.shape[0]
    send[...] = add(own[:half, :], got[:half, :]).astype(BF)
    keep[...] = add(own[half:, :], got[half:, :]).astype(BF)


def add(*terms):
    total = terms[0].astype(F32)
    for term in terms[1:]:
        total = total + term.astype(F32)
    return total


def middle_kernel(one, two, from_left, from_right, onward, backward):
    onward[...] = add(one[0], from_left[0]).astype(BF)
    backward[...] = add(two[0], from_right[0]).astype(BF)


def crossing_kernel(keep, got, end, out):
    out[...] = add(keep[1], got[1], end[...]).astype(BF)


def down_middle_kernel(keep, got, out):
    size = out.shape[0]
    out[...] = add(keep[:size, :], got[:size, :]).astype(BF)


def token_end_kernel(keep, got, end, last, out, ended):
    ended[...] = jnp.zeros_like(ended)
    out[...] = add(keep[1], got[1], end[...], last[...]).astype(BF)


def moment_step(old_value, column_total, count):
    return decay_rate * old_value + (1.0 - decay_rate) * (column_total / count + epsilon_one)


def row_totals(values):
    folded = values[:, :128]
    for k in range(1, values.shape[1] // 128):
        folded = folded + values[:, k * 128 : (k + 1) * 128]
    return jnp.sum(folded.T, axis=0, keepdims=True)


def down_rows(row):
    return jnp.broadcast_to(row, (128, row.shape[1])).T


def rows_kernel(keep, near_one, end, got, g_gate, g_up, pay):
    units = g_gate.shape[1]
    sums = []
    for k, out in enumerate((g_gate, g_up)):
        cols = pl.ds(k * units, units)
        g = add(keep[1, :, cols], near_one[1, :, cols], end[:, cols], got[:, cols])
        out[...] = g
        sums.append(row_totals(g * g))
    block = jnp.concatenate(sums + [jnp.zeros((6, 128), F32)], axis=0)
    for k in range(pay.shape[0]):
        pay[k] = block


def columns_kernel(
    counts, g_gate, g_up, keep, near_one, end, rows, row_gate, row_up, row_down,
    g_down, gate_new, up_new, down_new, pay, gate_out, up_out, down_out, work,
):
    all_units, width = counts
    size = g_down.shape[0]
    g_down[...] = add(keep[size:, :], near_one[size:, :], end[...])
    total = rows[0]
    for k in range(1, rows.shape[0]):
        total = total + rows[k]
    gate_new[...] = moment_step(row_gate[...], total[0:1, :], all_units)
    up_new[...] = moment_step(row_up[...], total[1:2, :], all_units)
    down = g_down[...]
    down_new[...] = moment_step(row_down[...], row_totals(down * down), width)
    gate_out[...] = gate_new[...]
    up_out[...] = up_new[...]
    down_out[...] = down_new[...]
    at = 0
    for g, new in ((g_gate, gate_new), (g_up, up_new), (g_down, down_new)):
        blocks = g.shape[1] // 128
        scale = 1.0 / down_rows(new[...])
        for k in range(blocks):
            value = g[:, k * 128 : (k + 1) * 128]
            square = value * value
            work[pl.ds(at + k, 1), :] = jnp.sum(square, axis=0, keepdims=True)
            work[pl.ds(at + blocks + k, 1), :] = jnp.sum(square * scale, axis=0, keepdims=True)
        at += 2 * blocks
    sums = jnp.concatenate(
        [
            jnp.broadcast_to(jnp.sum(new[...], axis=1, keepdims=True), (1, 128))
            for new in (gate_new, up_new, down_new)
        ]
        + [jnp.zeros((5, 128), F32)],
        axis=0,
    )
    high = sums.astype(BF).astype(F32)
    work[64:72, :] = high
    work[72:80, :] = sums - high
    block = work[...].astype(BF)
    for k in range(pay.shape[0]):
        pay[k] = block


def spread(value):
    return jnp.broadcast_to(
        jnp.sum(jnp.sum(value, axis=0, keepdims=True), axis=1, keepdims=True), (1, 128)
    )


def partial_kernel(width, got, col_gate, col_up, gate_new, up_new, sums, pay, gate_out, up_out):
    total = add(*[got[k] for k in range(got.shape[0])])
    row_sums = total[64:72] + total[72:80]
    gate = moment_step(col_gate[...], total[0:8], width)
    up = moment_step(col_up[...], total[16:24], width)
    gate_new[...] = gate
    up_new[...] = up
    gate_out[...] = gate
    up_out[...] = up
    sums[...] = row_sums
    for k in range(pay.shape[0]):
        pay[k, 0:32, :] = total[32:64]
        pay[k, 32:40, :] = jnp.concatenate(
            [
                spread(total[8:16] / gate),
                spread(total[24:32] / up),
                row_sums[2:3],
                jnp.zeros((5, 128), F32),
            ],
            axis=0,
        )


def update_kernel(
    counts, got, sums, col_down, g_gate, g_up, g_down, row_gate, row_up, row_down, col_gate, col_up,
    gate_out, up_out, down_out, down_new,
):
    all_units, width = counts
    total = got[0]
    for k in range(1, got.shape[0]):
        total = total + got[k]
    down = moment_step(col_down[...], total[0:16], all_units)
    down_new[...] = down
    entries = float(width * all_units)
    work = (
        (gate_out, g_gate, row_gate, col_gate[...], sums[0:1, :] / width, total[32:33]),
        (up_out, g_up, row_up, col_up[...], sums[1:2, :] / width, total[33:34]),
        (down_out, g_down, row_down, down, total[34:35] / all_units, spread(total[16:32] / down)),
    )
    for out, g, row, col, mean, squares in work:
        factor = jnp.sqrt(mean) / jnp.maximum(1.0, jnp.sqrt(mean * squares / entries))
        by_row = lax.rsqrt(down_rows(row[...]))
        by_col = lax.rsqrt(col) * factor
        for k in range(col.shape[0]):
            cols = pl.ds(k * 128, 128)
            out[:, cols] = g[:, cols] * by_row * by_col[k : k + 1, :]


def body(
    tokens, cotangent, w_gate, w_up, w_down, row_gate, col_gate, row_up, col_up, row_down, col_down
):
    rows, width = tokens.shape
    units = w_gate.shape[1]
    all_units = units * 8
    scale = float(rows * 16) ** (-0.5)
    dp, mp = lax.axis_index("dp"), lax.axis_index("mp")
    idx = jnp.stack([dp // 4, (dp // 2) % 2, dp % 2, mp // 2, mp % 2]).astype(jnp.int32)
    swap = dp_shift(dc=1)
    forth, back, across = dp_shift(dz=1), dp_shift(dz=3), dp_shift(dx=1)
    y_forth, y_back, x_across = mp_shift(dy=1), mp_shift(dy=3), mp_shift(dx=1)
    one = 2 * rows * width * units

    cot_peer = lax.ppermute(cotangent, "dp", swap)
    square = near((rows, units), F32)
    gate, tokens, w_gate, w_up = gate_pre(idx, tokens, w_gate, w_up)
    tok_peer = lax.ppermute(tokens, "dp", swap)
    hid = near((2, units // 4, rows), BF)
    act, slope, h_own, h_send = local_kernel(
        "up_pre", up_kernel, idx, [tokens, w_up, gate], [square, square, hid, hid], one
    )
    h_peer = lax.ppermute(h_send, "dp", swap)
    (grad,) = local_kernel(
        "hidden_grad", grad_kernel, None, [cotangent, w_down, act, slope],
        [near((2, rows, units), BF)], one,
        after=(tok_peer, cot_peer),
    )
    grad_peer = lax.ppermute(grad, "dp", swap)

    def down_part(side, after):
        return local_kernel(
            "down", functools.partial(down_kernel, side, scale), None,
            [h_own, h_peer, cotangent, cot_peer], [near((units // 4, width), BF)], one // 2,
            after=after,
        )[0]

    def weight_part(plan, after):
        out = near((2, width // 16, 2 * units), BF)
        return local_kernel(
            "weight", functools.partial(weight_kernel, plan, scale), idx,
            [tokens, tok_peer, grad, grad_peer], [out, out], one, after=after,
        )

    def token_part(plan, after):
        out = near((2, rows, width // 8), BF)
        return local_kernel(
            "token_grad", functools.partial(token_kernel, plan), idx, [grad, w_gate, w_up],
            [out, out], one, after=after,
        )

    tok_r, tok_l = token_part(FIRST, ())
    pair_r, pair_l = weight_part(FIRST, (tok_r,))
    away = down_part(0, (pair_r,))
    pair_a, pair_b = weight_part(SECOND, (away,))
    tok_a, tok_b = token_part(SECOND, (pair_a,))
    own = down_part(1, (tok_a,))

    def middle(parts, got, after):
        out = near(parts[0].shape[1:], BF)
        return local_kernel("middle", middle_kernel, None, [*parts, *got], [out, out], 1000,
                            after=after)

    def crossing(keep, got, end, after):
        out = near(end.shape, BF)
        return local_kernel("crossing", crossing_kernel, None, [keep, got, end], [out], 1000,
                            after=after)[0]

    tok_got = lax.ppermute(tok_r, "mp", y_forth), lax.ppermute(tok_l, "mp", y_back)
    tok_mid = middle((tok_a, tok_b), tok_got, (own,))
    tok_end = lax.ppermute(tok_mid[0], "mp", y_forth), lax.ppermute(tok_mid[1], "mp", y_back)
    pair_got = lax.ppermute(pair_r, "dp", forth), lax.ppermute(pair_l, "dp", back)
    pair_mid = middle((pair_a, pair_b), pair_got, (tok_mid[0],))
    pair_end = lax.ppermute(pair_mid[0], "dp", forth), lax.ppermute(pair_mid[1], "dp", back)
    tok_away = crossing(tok_a, tok_got[1], tok_end[0], (pair_mid[0], tok_end[1]))
    tok_last = lax.ppermute(tok_away, "mp", x_across)
    part = near((units // 8, width), BF)
    down_away, down_keep = local_kernel(
        "down_mix", mix_kernel, None, [own, lax.ppermute(away, "dp", across)], [part] * 2, 1000,
        after=(tok_away,),
    )
    down_got = lax.ppermute(down_away, "dp", dp_pairs(1))
    pair_away = crossing(pair_a, pair_got[1], pair_end[0], (down_away, pair_end[1], tok_last))
    pair_last = lax.ppermute(pair_away, "dp", across)
    (down_mid,) = local_kernel(
        "down_middle", down_middle_kernel, None, [down_keep, down_got],
        [near((units // 16, width), BF)], 1000, after=(pair_away,),
    )
    down_end = lax.ppermute(down_mid, "dp", dp_pairs(3))
    token_grad, tok_ended = local_kernel(
        "token_end", token_end_kernel, None, [tok_b, tok_got[0], tok_end[1], tok_last],
        [jax.ShapeDtypeStruct((rows, width // 8), BF), near((8, 128), F32)], 1000,
        after=(down_mid,),
    )

    shard = near((width // 16, units), F32)
    g_gate, g_up, pay = local_kernel(
        "row_sums", rows_kernel, None,
        [pair_b, pair_got[0], pair_end[1], pair_last],
        [shard, shard, near((8, 8, 128), F32)], 1000, after=(tok_ended,), limit=4,
    )
    row_got = lax.all_to_all(pay, "mp", 0, 0, tiled=True)

    counts = (all_units, width)
    line = near((1, width // 16), F32)
    short = near((1, units // 16), F32)
    line_out = jax.ShapeDtypeStruct((1, width // 16), F32)
    short_out = jax.ShapeDtypeStruct((1, units // 16), F32)
    g_down, row_gate_new, row_up_new, row_down_new, pay, *rows_out, _ = local_kernel(
        "column_sums", functools.partial(columns_kernel, counts), None,
        [
            g_gate, g_up, down_keep, down_got, down_end, row_got,
            row_gate.reshape(1, -1), row_up.reshape(1, -1), row_down.reshape(1, -1),
        ],
        [near((units // 16, width), F32), line, line, short, near((16, 80, 128), BF),
         line_out, line_out, short_out, near((80, 128), F32)],
        1000, limit=4,
    )
    col_got = lax.all_to_all(pay, "dp", 0, 0, tiled=True)

    lines = near((units // 128, 128), F32)
    lines_out = jax.ShapeDtypeStruct((units // 128, 128), F32)
    col_gate_new, col_up_new, sums, pay, *cols_out = local_kernel(
        "partial_sums", functools.partial(partial_kernel, width), None,
        [col_got, col_gate.reshape(-1, 128), col_up.reshape(-1, 128)],
        [lines, lines, near((8, 128), F32), near((8, 40, 128), F32), lines_out, lines_out], 1000, limit=4,
    )
    last = lax.all_to_all(pay, "mp", 0, 0, tiled=True)
    update_gate, update_up, update_down, col_down_new = local_kernel(
        "updates", functools.partial(update_kernel, counts), None,
        [
            last, sums, col_down.reshape(-1, 128), g_gate, g_up, g_down,
            row_gate_new, row_up_new, row_down_new, col_gate_new, col_up_new,
        ],
        [
            jax.ShapeDtypeStruct((width // 16, units), F32),
            jax.ShapeDtypeStruct((width // 16, units), F32),
            jax.ShapeDtypeStruct((units // 16, width), F32),
            jax.ShapeDtypeStruct((width // 128, 128), F32),
        ],
        1000, limit=8,
    )
    return (
        token_grad,
        update_gate,
        update_up,
        update_down,
        rows_out[0].reshape(-1),
        cols_out[0].reshape(-1),
        rows_out[1].reshape(-1),
        cols_out[1].reshape(-1),
        rows_out[2].reshape(-1),
        col_down_new.reshape(-1),
    )


def solution(mesh):
    in_specs = (
        P("dp", None),
        P("dp", None),
        P(None, "mp"),
        P(None, "mp"),
        P("mp", None),
        P("dp"),
        P("mp"),
        P("dp"),
        P("mp"),
        P(("mp", "dp")),
        P(),
    )
    out_specs = (
        P("dp", "mp"),
        P("dp", "mp"),
        P("dp", "mp"),
        P(("mp", "dp"), None),
        P("dp"),
        P("mp"),
        P("dp"),
        P("mp"),
        P(("mp", "dp")),
        P(),
    )
    return jax.shard_map(body, mesh=mesh, in_specs=in_specs, out_specs=out_specs, check_vma=False)
```

```python
import functools

import jax
import jax.numpy as jnp
from jax import lax
from jax.experimental import pallas as pl
from jax.experimental.pallas import tpu as pltpu
from jax.sharding import PartitionSpec as P

epsilon_one = 1e-30
decay_rate = 0.8
BF = jnp.bfloat16
F32 = jnp.float32
MIB = 1024 * 1024
EARLY = 16
FIRST = (((2, 0), (2, 1)), ((1, 1), (3, 0)))
SECOND = (((1, 0), (3, 1)), ((0, 0), (0, 1)))


def dp_shift(dz=0, dx=0, dc=0):
    pairs = []
    for z in range(4):
        for x in range(2):
            for c in range(2):
                to = ((z + dz) % 4) * 4 + (x ^ dx) * 2 + (c ^ dc)
                pairs.append((z * 4 + x * 2 + c, to))
    return pairs


def dp_pairs(flip):
    return [(k, (((k // 4) ^ flip) * 4) + k % 4) for k in range(16)]


def mp_shift(dy=0, dx=0):
    return [(y * 2 + x, ((y + dy) % 4) * 2 + (x ^ dx)) for y in range(4) for x in range(2)]


def contract(a, b, dim_a, dim_b):
    return lax.dot_general(a, b, (((dim_a,), (dim_b,)), ((), ())), preferred_element_type=F32)


def local_kernel(name, kernel, scalars, arrays, outs, flops, after=(), limit=6):
    vmem = pl.BlockSpec(memory_space=pltpu.VMEM)
    count, late = len(arrays), len(after)

    def run(*refs):
        first = 0 if scalars is None else 1
        kernel(*refs[: first + count], *refs[first + count + late :])

    specs = [] if scalars is None else [pl.BlockSpec(memory_space=pltpu.SMEM)]
    operands = [] if scalars is None else [scalars]
    return pl.pallas_call(
        run,
        in_specs=specs + [vmem] * count + [pl.BlockSpec(memory_space=pl.ANY)] * late,
        out_specs=[vmem] * len(outs),
        out_shape=outs,
        compiler_params=pltpu.CompilerParams(vmem_limit_bytes=limit * MIB),
        cost_estimate=pl.CostEstimate(flops=flops // EARLY, bytes_accessed=1024, transcendentals=0),
        name=name,
    )(
        *operands,
        *[pltpu.with_memory_space_constraint(a, pltpu.VMEM) for a in arrays],
        *after,
    )


def near(shape, dtype):
    return pltpu.VMEM(shape, dtype)


def gate_kernel(idx, tok_in, wg_in, wu_in, gate, tok, wg, wu, tok_sem, wg_sem, wu_sem):
    rows = [pl.ds(m * 256, 256) for m in range(3)]
    deep = [pl.ds(n * 256, 256) for n in range(8)]
    wg_copy = [pltpu.make_async_copy(wg_in.at[d, :], wg.at[d, :], wg_sem.at[n])
               for n, d in enumerate(deep)]
    tok_copy = [pltpu.make_async_copy(tok_in.at[r, :], tok.at[r, :], tok_sem.at[m])
                for m, r in enumerate(rows)]
    wu_copy = pltpu.make_async_copy(wu_in, wu, wu_sem)
    for copy in (tok_copy[0], *wg_copy[:4], *tok_copy[1:], *wg_copy[4:], wu_copy):
        copy.start()
    for half in range(2):
        depth = pl.ds(half * 1024, 1024)
        for copy in wg_copy[half * 4 : half * 4 + 4]:
            copy.wait()
        for m, r in enumerate(rows):
            if half == 0:
                tok_copy[m].wait()
            for n in range(2):
                c = pl.ds(n * 512, 512)
                term = contract(tok[r, depth], wg[depth, c], 1, 0)
                gate[r, c] = term if half == 0 else gate[r, c] + term
    wu_copy.wait()


def gate_pre(idx, tokens, w_gate, w_up):
    vmem, hbm = pl.BlockSpec(memory_space=pltpu.VMEM), pl.BlockSpec(memory_space=pltpu.HBM)
    rows, width = tokens.shape
    units = w_gate.shape[1]
    return pl.pallas_call(
        gate_kernel,
        in_specs=[pl.BlockSpec(memory_space=pltpu.SMEM), hbm, hbm, hbm],
        out_specs=[vmem] * 4,
        out_shape=[near((rows, units), F32), near(tokens.shape, BF), near(w_gate.shape, BF),
                   near(w_up.shape, BF)],
        scratch_shapes=[pltpu.SemaphoreType.DMA((3,)), pltpu.SemaphoreType.DMA((8,)),
                        pltpu.SemaphoreType.DMA],
        compiler_params=pltpu.CompilerParams(vmem_limit_bytes=4 * MIB),
        cost_estimate=pl.CostEstimate(flops=1000000, bytes_accessed=1024, transcendentals=0),
        name="gate_pre",
    )(idx, *[pltpu.with_memory_space_constraint(a, pltpu.HBM) for a in (tokens, w_gate, w_up)])


def up_kernel(idx, tok, wu, gate, act_out, slope_out, h_own, h_send):
    z, xh, core = idx[0], idx[1], idx[2]
    for r, far in enumerate((2, 1, 3, 0)):
        cols = pl.ds(pl.multiple_of(lax.bitwise_xor(z, far) * 256, 256), 256)
        pre = gate[:, cols]
        up = contract(tok[...], wu[:, cols], 1, 0)
        sig = 1.0 / (1.0 + jnp.exp(-pre))
        act = pre * sig
        act_out[:, cols] = act
        slope_out[:, cols] = up * (sig * (1.0 + pre * (1.0 - sig)))
        hid = (act * up).astype(BF).T
        piece = [hid[k * 64 : (k + 1) * 64, :] for k in range(4)]
        own = [jnp.where(core == 0, piece[2 * a], piece[2 * a + 1]) for a in range(2)]
        send = [jnp.where(core == 0, piece[2 * a + 1], piece[2 * a]) for a in range(2)]
        rows = pl.ds(r * 64, 64)
        for ref, pair in ((h_own, own), (h_send, send)):
            ref[0, rows, :] = jnp.where(xh == 0, pair[1], pair[0])
            ref[1, rows, :] = jnp.where(xh == 0, pair[0], pair[1])


def grad_kernel(cot, wd, act, slope, out):
    for j in range(4):
        cols = pl.ds(j * 256, 256)
        grad = contract(cot[...], wd[cols, :], 1, 1)
        out[0, :, cols] = (grad * slope[:, cols]).astype(BF)
        out[1, :, cols] = (grad * act[:, cols]).astype(BF)


def down_kernel(side, scale, h_own, h_peer, cot, cot_peer, out):
    for j in range(4):
        cols = pl.ds(j * 512, 512)
        term = contract(h_own[side], cot[:, cols], 1, 0)
        term = term + contract(h_peer[side], cot_peer[:, cols], 1, 0)
        out[:, cols] = (term * scale).astype(BF)


def weight_kernel(plan, scale, idx, tok, tok_peer, grad, grad_peer, one, two):
    z, xh, core = idx[0], idx[1], idx[2]

    def block(ref, r, side):
        x = xh if side == 1 else 1 - xh
        at = ((lax.rem(z + r, 4) * 2 + x) * 2 + core) * 128
        return ref[:, pl.ds(pl.multiple_of(at, 128), 128)]

    for k in range(2):
        mine, theirs = (
            jnp.concatenate([block(ref, *plan[k][0]), block(ref, *plan[k][1])], axis=1)
            for ref in (tok, tok_peer)
        )
        for j in range(4):
            cols, to = pl.ds((j % 2) * 512, 512), pl.ds(j * 512, 512)
            term = contract(mine, grad[j // 2, :, cols], 0, 0)
            term = (term + contract(theirs, grad_peer[j // 2, :, cols], 0, 0)) * scale
            one[k, :, to] = term[:128, :].astype(BF)
            two[k, :, to] = term[128:, :].astype(BF)


def token_kernel(plan, idx, grad, wg, wu, one, two):
    y, xl = idx[3], idx[4]
    for k in range(2):
        for out, (r, side) in zip((one, two), plan[k]):
            x = xl if side == 1 else 1 - xl
            at = (lax.rem(y + r, 4) * 2 + x) * 256
            rows = pl.ds(pl.multiple_of(at, 256), 256)
            term = contract(grad[0], wg[rows, :], 1, 1) + contract(grad[1], wu[rows, :], 1, 1)
            out[k] = term.astype(BF)


def mix_kernel(own, got, send, keep):
    half = send.shape[0]
    send[...] = add(own[:half, :], got[:half, :]).astype(BF)
    keep[...] = add(own[half:, :], got[half:, :]).astype(BF)


def add(*terms):
    total = terms[0].astype(F32)
    for term in terms[1:]:
        total = total + term.astype(F32)
    return total


def middle_kernel(one, two, from_left, from_right, onward, backward):
    onward[...] = add(one[0], from_left[0]).astype(BF)
    backward[...] = add(two[0], from_right[0]).astype(BF)


def crossing_kernel(keep, got, end, out):
    out[...] = add(keep[1], got[1], end[...]).astype(BF)


def down_middle_kernel(keep, got, out):
    size = out.shape[0]
    out[...] = add(keep[:size, :], got[:size, :]).astype(BF)


def token_end_kernel(keep, got, end, last, out, ended):
    ended[...] = jnp.zeros_like(ended)
    out[...] = add(keep[1], got[1], end[...], last[...]).astype(BF)


def moment_step(old_value, column_total, count):
    return decay_rate * old_value + (1.0 - decay_rate) * (column_total / count + epsilon_one)


def row_totals(values):
    folded = values[:, :128]
    for k in range(1, values.shape[1] // 128):
        folded = folded + values[:, k * 128 : (k + 1) * 128]
    return jnp.sum(folded.T, axis=0, keepdims=True)


def down_rows(row):
    return jnp.broadcast_to(row, (128, row.shape[1])).T


def rows_kernel(keep, near_one, end, got, g_gate, g_up, pay):
    units = g_gate.shape[1]
    sums = []
    for k, out in enumerate((g_gate, g_up)):
        cols = pl.ds(k * units, units)
        g = add(keep[1, :, cols], near_one[1, :, cols], end[:, cols], got[:, cols])
        out[...] = g
        sums.append(row_totals(g * g))
    block = jnp.concatenate(sums + [jnp.zeros((6, 128), F32)], axis=0)
    for k in range(pay.shape[0]):
        pay[k] = block


def columns_kernel(
    counts, g_gate, g_up, keep, near_one, end, rows, row_gate, row_up, row_down,
    g_down, gate_new, up_new, down_new, pay, gate_out, up_out, down_out, work,
):
    all_units, width = counts
    size = g_down.shape[0]
    g_down[...] = add(keep[size:, :], near_one[size:, :], end[...])
    total = rows[0]
    for k in range(1, rows.shape[0]):
        total = total + rows[k]
    gate_new[...] = moment_step(row_gate[...], total[0:1, :], all_units)
    up_new[...] = moment_step(row_up[...], total[1:2, :], all_units)
    down = g_down[...]
    down_new[...] = moment_step(row_down[...], row_totals(down * down), width)
    gate_out[...] = gate_new[...]
    up_out[...] = up_new[...]
    down_out[...] = down_new[...]
    at = 0
    for g, new in ((g_gate, gate_new), (g_up, up_new), (g_down, down_new)):
        blocks = g.shape[1] // 128
        scale = 1.0 / down_rows(new[...])
        for k in range(blocks):
            value = g[:, k * 128 : (k + 1) * 128]
            square = value * value
            work[pl.ds(at + k, 1), :] = jnp.sum(square, axis=0, keepdims=True)
            work[pl.ds(at + blocks + k, 1), :] = jnp.sum(square * scale, axis=0, keepdims=True)
        at += 2 * blocks
    sums = jnp.concatenate(
        [
            jnp.broadcast_to(jnp.sum(new[...], axis=1, keepdims=True), (1, 128))
            for new in (gate_new, up_new, down_new)
        ]
        + [jnp.zeros((5, 128), F32)],
        axis=0,
    )
    high = sums.astype(BF).astype(F32)
    work[64:72, :] = high
    work[72:80, :] = sums - high
    block = work[...].astype(BF)
    for k in range(pay.shape[0]):
        pay[k] = block


def spread(value):
    return jnp.broadcast_to(
        jnp.sum(jnp.sum(value, axis=0, keepdims=True), axis=1, keepdims=True), (1, 128)
    )


def partial_kernel(width, got, col_gate, col_up, gate_new, up_new, sums, pay, gate_out, up_out):
    total = add(*[got[k] for k in range(got.shape[0])])
    row_sums = total[64:72] + total[72:80]
    gate = moment_step(col_gate[...], total[0:8], width)
    up = moment_step(col_up[...], total[16:24], width)
    gate_new[...] = gate
    up_new[...] = up
    gate_out[...] = gate
    up_out[...] = up
    sums[...] = row_sums
    for k in range(pay.shape[0]):
        pay[k, 0:32, :] = total[32:64]
        pay[k, 32:40, :] = jnp.concatenate(
            [
                spread(total[8:16] / gate),
                spread(total[24:32] / up),
                row_sums[2:3],
                jnp.zeros((5, 128), F32),
            ],
            axis=0,
        )


def update_kernel(
    counts, got, sums, col_down, g_gate, g_up, g_down, row_gate, row_up, row_down, col_gate, col_up,
    gate_out, up_out, down_out, down_new,
):
    all_units, width = counts
    total = got[0]
    for k in range(1, got.shape[0]):
        total = total + got[k]
    down = moment_step(col_down[...], total[0:16], all_units)
    down_new[...] = down
    entries = float(width * all_units)
    work = (
        (gate_out, g_gate, row_gate, col_gate[...], sums[0:1, :] / width, total[32:33]),
        (up_out, g_up, row_up, col_up[...], sums[1:2, :] / width, total[33:34]),
        (down_out, g_down, row_down, down, total[34:35] / all_units, spread(total[16:32] / down)),
    )
    for out, g, row, col, mean, squares in work:
        factor = jnp.sqrt(mean) / jnp.maximum(1.0, jnp.sqrt(mean * squares / entries))
        by_row = lax.rsqrt(down_rows(row[...]))
        by_col = lax.rsqrt(col) * factor
        for k in range(col.shape[0]):
            cols = pl.ds(k * 128, 128)
            out[:, cols] = g[:, cols] * by_row * by_col[k : k + 1, :]


def body(
    tokens, cotangent, w_gate, w_up, w_down, row_gate, col_gate, row_up, col_up, row_down, col_down
):
    rows, width = tokens.shape
    units = w_gate.shape[1]
    all_units = units * 8
    scale = float(rows * 16) ** (-0.5)
    dp, mp = lax.axis_index("dp"), lax.axis_index("mp")
    idx = jnp.stack([dp // 4, (dp // 2) % 2, dp % 2, mp // 2, mp % 2]).astype(jnp.int32)
    swap = dp_shift(dc=1)
    forth, back, across = dp_shift(dz=1), dp_shift(dz=3), dp_shift(dx=1)
    y_forth, y_back, x_across = mp_shift(dy=1), mp_shift(dy=3), mp_shift(dx=1)
    one = 2 * rows * width * units

    cot_peer = lax.ppermute(cotangent, "dp", swap)
    square = near((rows, units), F32)
    gate, tokens, w_gate, w_up = gate_pre(idx, tokens, w_gate, w_up)
    tok_peer = lax.ppermute(tokens, "dp", swap)
    hid = near((2, units // 4, rows), BF)
    act, slope, h_own, h_send = local_kernel(
        "up_pre", up_kernel, idx, [tokens, w_up, gate], [square, square, hid, hid], one
    )
    h_peer = lax.ppermute(h_send, "dp", swap)
    (grad,) = local_kernel(
        "hidden_grad", grad_kernel, None, [cotangent, w_down, act, slope],
        [near((2, rows, units), BF)], one,
        after=(tok_peer, cot_peer),
    )
    grad_peer = lax.ppermute(grad, "dp", swap)

    def down_part(side, after):
        return local_kernel(
            "down", functools.partial(down_kernel, side, scale), None,
            [h_own, h_peer, cotangent, cot_peer], [near((units // 4, width), BF)], one // 2,
            after=after,
        )[0]

    def weight_part(plan, after):
        out = near((2, width // 16, 2 * units), BF)
        return local_kernel(
            "weight", functools.partial(weight_kernel, plan, scale), idx,
            [tokens, tok_peer, grad, grad_peer], [out, out], one, after=after,
        )

    def token_part(plan, after):
        out = near((2, rows, width // 8), BF)
        return local_kernel(
            "token_grad", functools.partial(token_kernel, plan), idx, [grad, w_gate, w_up],
            [out, out], one, after=after,
        )

    tok_r, tok_l = token_part(FIRST, ())
    pair_r, pair_l = weight_part(FIRST, (tok_r,))
    away = down_part(0, (pair_r,))
    pair_a, pair_b = weight_part(SECOND, (away,))
    tok_a, tok_b = token_part(SECOND, (pair_a,))
    own = down_part(1, (tok_a,))

    def middle(parts, got, after):
        out = near(parts[0].shape[1:], BF)
        return local_kernel("middle", middle_kernel, None, [*parts, *got], [out, out], 1000,
                            after=after)

    def crossing(keep, got, end, after):
        out = near(end.shape, BF)
        return local_kernel("crossing", crossing_kernel, None, [keep, got, end], [out], 1000,
                            after=after)[0]

    tok_got = lax.ppermute(tok_r, "mp", y_forth), lax.ppermute(tok_l, "mp", y_back)
    tok_mid = middle((tok_a, tok_b), tok_got, (own,))
    tok_end = lax.ppermute(tok_mid[0], "mp", y_forth), lax.ppermute(tok_mid[1], "mp", y_back)
    pair_got = lax.ppermute(pair_r, "dp", forth), lax.ppermute(pair_l, "dp", back)
    pair_mid = middle((pair_a, pair_b), pair_got, (tok_mid[0],))
    pair_end = lax.ppermute(pair_mid[0], "dp", forth), lax.ppermute(pair_mid[1], "dp", back)
    tok_away = crossing(tok_a, tok_got[1], tok_end[0], (pair_mid[0], tok_end[1]))
    tok_last = lax.ppermute(tok_away, "mp", x_across)
    part = near((units // 8, width), BF)
    down_away, down_keep = local_kernel(
        "down_mix", mix_kernel, None, [own, lax.ppermute(away, "dp", across)], [part] * 2, 1000,
        after=(tok_away,),
    )
    down_got = lax.ppermute(down_away, "dp", dp_pairs(1))
    pair_away = crossing(pair_a, pair_got[1], pair_end[0], (down_away, pair_end[1], tok_last))
    pair_last = lax.ppermute(pair_away, "dp", across)
    (down_mid,) = local_kernel(
        "down_middle", down_middle_kernel, None, [down_keep, down_got],
        [near((units // 16, width), BF)], 1000, after=(pair_away,),
    )
    down_end = lax.ppermute(down_mid, "dp", dp_pairs(3))
    token_grad, tok_ended = local_kernel(
        "token_end", token_end_kernel, None, [tok_b, tok_got[0], tok_end[1], tok_last],
        [jax.ShapeDtypeStruct((rows, width // 8), BF), near((8, 128), F32)], 1000,
        after=(down_mid,),
    )

    shard = near((width // 16, units), F32)
    g_gate, g_up, pay = local_kernel(
        "row_sums", rows_kernel, None,
        [pair_b, pair_got[0], pair_end[1], pair_last],
        [shard, shard, near((8, 8, 128), F32)], 1000, after=(tok_ended,), limit=4,
    )
    row_got = lax.all_to_all(pay, "mp", 0, 0, tiled=True)

    counts = (all_units, width)
    line = near((1, width // 16), F32)
    short = near((1, units // 16), F32)
    line_out = jax.ShapeDtypeStruct((1, width // 16), F32)
    short_out = jax.ShapeDtypeStruct((1, units // 16), F32)
    g_down, row_gate_new, row_up_new, row_down_new, pay, *rows_out, _ = local_kernel(
        "column_sums", functools.partial(columns_kernel, counts), None,
        [
            g_gate, g_up, down_keep, down_got, down_end, row_got,
            row_gate.reshape(1, -1), row_up.reshape(1, -1), row_down.reshape(1, -1),
        ],
        [near((units // 16, width), F32), line, line, short, near((16, 80, 128), BF),
         line_out, line_out, short_out, near((80, 128), F32)],
        1000, limit=4,
    )
    col_got = lax.all_to_all(pay, "dp", 0, 0, tiled=True)

    lines = near((units // 128, 128), F32)
    lines_out = jax.ShapeDtypeStruct((units // 128, 128), F32)
    col_gate_new, col_up_new, sums, pay, *cols_out = local_kernel(
        "partial_sums", functools.partial(partial_kernel, width), None,
        [col_got, col_gate.reshape(-1, 128), col_up.reshape(-1, 128)],
        [lines, lines, near((8, 128), F32), near((8, 40, 128), F32), lines_out, lines_out], 1000, limit=4,
    )
    last = lax.all_to_all(pay, "mp", 0, 0, tiled=True)
    update_gate, update_up, update_down, col_down_new = local_kernel(
        "updates", functools.partial(update_kernel, counts), None,
        [
            last, sums, col_down.reshape(-1, 128), g_gate, g_up, g_down,
            row_gate_new, row_up_new, row_down_new, col_gate_new, col_up_new,
        ],
        [
            jax.ShapeDtypeStruct((width // 16, units), F32),
            jax.ShapeDtypeStruct((width // 16, units), F32),
            jax.ShapeDtypeStruct((units // 16, width), F32),
            jax.ShapeDtypeStruct((width // 128, 128), F32),
        ],
        1000, limit=8,
    )
    return (
        token_grad,
        update_gate,
        update_up,
        update_down,
        rows_out[0].reshape(-1),
        cols_out[0].reshape(-1),
        rows_out[1].reshape(-1),
        cols_out[1].reshape(-1),
        rows_out[2].reshape(-1),
        col_down_new.reshape(-1),
    )


def solution(mesh):
    in_specs = (
        P("dp", None),
        P("dp", None),
        P(None, "mp"),
        P(None, "mp"),
        P("mp", None),
        P("dp"),
        P("mp"),
        P("dp"),
        P("mp"),
        P(("mp", "dp")),
        P(),
    )
    out_specs = (
        P("dp", "mp"),
        P("dp", "mp"),
        P("dp", "mp"),
        P(("mp", "dp"), None),
        P("dp"),
        P("mp"),
        P("dp"),
        P("mp"),
        P(("mp", "dp")),
        P(),
    )
    return jax.shard_map(body, mesh=mesh, in_specs=in_specs, out_specs=out_specs, check_vma=False)
```

```python
import functools

import jax
import jax.numpy as jnp
from jax import lax
from jax.experimental import pallas as pl
from jax.experimental.pallas import tpu as pltpu
from jax.sharding import PartitionSpec as P

epsilon_one = 1e-30
decay_rate = 0.8
BF = jnp.bfloat16
F32 = jnp.float32
MIB = 1024 * 1024
EARLY = 16
FIRST = (((2, 0), (2, 1)), ((1, 1), (3, 0)))
SECOND = (((1, 0), (3, 1)), ((0, 0), (0, 1)))


def dp_shift(dz=0, dx=0, dc=0):
    pairs = []
    for z in range(4):
        for x in range(2):
            for c in range(2):
                to = ((z + dz) % 4) * 4 + (x ^ dx) * 2 + (c ^ dc)
                pairs.append((z * 4 + x * 2 + c, to))
    return pairs


def dp_pairs(flip):
    return [(k, (((k // 4) ^ flip) * 4) + k % 4) for k in range(16)]


def mp_shift(dy=0, dx=0):
    return [(y * 2 + x, ((y + dy) % 4) * 2 + (x ^ dx)) for y in range(4) for x in range(2)]


def contract(a, b, dim_a, dim_b):
    return lax.dot_general(a, b, (((dim_a,), (dim_b,)), ((), ())), preferred_element_type=F32)


def local_kernel(name, kernel, scalars, arrays, outs, flops, after=(), limit=6):
    vmem = pl.BlockSpec(memory_space=pltpu.VMEM)
    count, late = len(arrays), len(after)

    def run(*refs):
        first = 0 if scalars is None else 1
        kernel(*refs[: first + count], *refs[first + count + late :])

    specs = [] if scalars is None else [pl.BlockSpec(memory_space=pltpu.SMEM)]
    operands = [] if scalars is None else [scalars]
    return pl.pallas_call(
        run,
        in_specs=specs + [vmem] * count + [pl.BlockSpec(memory_space=pl.ANY)] * late,
        out_specs=[vmem] * len(outs),
        out_shape=outs,
        compiler_params=pltpu.CompilerParams(vmem_limit_bytes=limit * MIB),
        cost_estimate=pl.CostEstimate(flops=flops // EARLY, bytes_accessed=1024, transcendentals=0),
        name=name,
    )(
        *operands,
        *[pltpu.with_memory_space_constraint(a, pltpu.VMEM) for a in arrays],
        *after,
    )


def near(shape, dtype):
    return pltpu.VMEM(shape, dtype)


def gate_kernel(idx, tok_in, wg_in, wu_in, gate, tok, wg, wu, tok_sem, wg_sem, wu_sem):
    rows = [pl.ds(m * 256, 256) for m in range(3)]
    deep = [pl.ds(n * 256, 256) for n in range(8)]
    wg_copy = [pltpu.make_async_copy(wg_in.at[d, :], wg.at[d, :], wg_sem.at[n])
               for n, d in enumerate(deep)]
    tok_copy = [pltpu.make_async_copy(tok_in.at[r, :], tok.at[r, :], tok_sem.at[m])
                for m, r in enumerate(rows)]
    wu_copy = pltpu.make_async_copy(wu_in, wu, wu_sem)
    for copy in (tok_copy[0], *wg_copy[:4], *tok_copy[1:], *wg_copy[4:], wu_copy):
        copy.start()
    for half in range(2):
        depth = pl.ds(half * 1024, 1024)
        for copy in wg_copy[half * 4 : half * 4 + 4]:
            copy.wait()
        for m, r in enumerate(rows):
            if half == 0:
                tok_copy[m].wait()
            for n in range(2):
                c = pl.ds(n * 512, 512)
                term = contract(tok[r, depth], wg[depth, c], 1, 0)
                gate[r, c] = term if half == 0 else gate[r, c] + term
    wu_copy.wait()


def gate_pre(idx, tokens, w_gate, w_up):
    vmem, hbm = pl.BlockSpec(memory_space=pltpu.VMEM), pl.BlockSpec(memory_space=pltpu.HBM)
    rows, width = tokens.shape
    units = w_gate.shape[1]
    return pl.pallas_call(
        gate_kernel,
        in_specs=[pl.BlockSpec(memory_space=pltpu.SMEM), hbm, hbm, hbm],
        out_specs=[vmem] * 4,
        out_shape=[near((rows, units), F32), near(tokens.shape, BF), near(w_gate.shape, BF),
                   near(w_up.shape, BF)],
        scratch_shapes=[pltpu.SemaphoreType.DMA((3,)), pltpu.SemaphoreType.DMA((8,)),
                        pltpu.SemaphoreType.DMA],
        compiler_params=pltpu.CompilerParams(vmem_limit_bytes=4 * MIB),
        cost_estimate=pl.CostEstimate(flops=1000000, bytes_accessed=1024, transcendentals=0),
        name="gate_pre",
    )(idx, *[pltpu.with_memory_space_constraint(a, pltpu.HBM) for a in (tokens, w_gate, w_up)])


def up_kernel(idx, tok, wu, gate, act_out, slope_out, h_own, h_send):
    z, xh, core = idx[0], idx[1], idx[2]
    for r, far in enumerate((2, 1, 3, 0)):
        cols = pl.ds(pl.multiple_of(lax.bitwise_xor(z, far) * 256, 256), 256)
        pre = gate[:, cols]
        up = contract(tok[...], wu[:, cols], 1, 0)
        sig = 1.0 / (1.0 + jnp.exp(-pre))
        act = pre * sig
        act_out[:, cols] = act
        slope_out[:, cols] = up * (sig * (1.0 + pre * (1.0 - sig)))
        hid = (act * up).astype(BF).T
        piece = [hid[k * 64 : (k + 1) * 64, :] for k in range(4)]
        own = [jnp.where(core == 0, piece[2 * a], piece[2 * a + 1]) for a in range(2)]
        send = [jnp.where(core == 0, piece[2 * a + 1], piece[2 * a]) for a in range(2)]
        rows = pl.ds(r * 64, 64)
        for ref, pair in ((h_own, own), (h_send, send)):
            ref[0, rows, :] = jnp.where(xh == 0, pair[1], pair[0])
            ref[1, rows, :] = jnp.where(xh == 0, pair[0], pair[1])


def grad_kernel(cot, wd, act, slope, out):
    for j in range(4):
        cols = pl.ds(j * 256, 256)
        grad = contract(cot[...], wd[cols, :], 1, 1)
        out[0, :, cols] = (grad * slope[:, cols]).astype(BF)
        out[1, :, cols] = (grad * act[:, cols]).astype(BF)


def down_kernel(side, scale, h_own, h_peer, cot, cot_peer, out):
    for j in range(4):
        cols = pl.ds(j * 512, 512)
        term = contract(h_own[side], cot[:, cols], 1, 0)
        term = term + contract(h_peer[side], cot_peer[:, cols], 1, 0)
        out[:, cols] = (term * scale).astype(BF)


def weight_kernel(plan, scale, idx, tok, tok_peer, grad, grad_peer, one, two):
    z, xh, core = idx[0], idx[1], idx[2]

    def block(ref, r, side):
        x = xh if side == 1 else 1 - xh
        at = ((lax.rem(z + r, 4) * 2 + x) * 2 + core) * 128
        return ref[:, pl.ds(pl.multiple_of(at, 128), 128)]

    for k in range(2):
        mine, theirs = (
            jnp.concatenate([block(ref, *plan[k][0]), block(ref, *plan[k][1])], axis=1)
            for ref in (tok, tok_peer)
        )
        for j in range(4):
            cols, to = pl.ds((j % 2) * 512, 512), pl.ds(j * 512, 512)
            term = contract(mine, grad[j // 2, :, cols], 0, 0)
            term = (term + contract(theirs, grad_peer[j // 2, :, cols], 0, 0)) * scale
            one[k, :, to] = term[:128, :].astype(BF)
            two[k, :, to] = term[128:, :].astype(BF)


def token_kernel(plan, idx, grad, wg, wu, one, two):
    y, xl = idx[3], idx[4]
    for k in range(2):
        for out, (r, side) in zip((one, two), plan[k]):
            x = xl if side == 1 else 1 - xl
            at = (lax.rem(y + r, 4) * 2 + x) * 256
            rows = pl.ds(pl.multiple_of(at, 256), 256)
            term = contract(grad[0], wg[rows, :], 1, 1) + contract(grad[1], wu[rows, :], 1, 1)
            out[k] = term.astype(BF)


def mix_kernel(own, got, send, keep):
    half = send.shape[0]
    send[...] = add(own[:half, :], got[:half, :]).astype(BF)
    keep[...] = add(own[half:, :], got[half:, :]).astype(BF)


def add(*terms):
    total = terms[0].astype(F32)
    for term in terms[1:]:
        total = total + term.astype(F32)
    return total


def middle_kernel(one, two, from_left, from_right, onward, backward):
    onward[...] = add(one[0], from_left[0]).astype(BF)
    backward[...] = add(two[0], from_right[0]).astype(BF)


def crossing_kernel(keep, got, end, out):
    out[...] = add(keep[1], got[1], end[...]).astype(BF)


def down_middle_kernel(keep, got, out):
    size = out.shape[0]
    out[...] = add(keep[:size, :], got[:size, :]).astype(BF)


def token_end_kernel(keep, got, end, last, out, ended):
    ended[...] = jnp.zeros_like(ended)
    out[...] = add(keep[1], got[1], end[...], last[...]).astype(BF)


def moment_step(old_value, column_total, count):
    return decay_rate * old_value + (1.0 - decay_rate) * (column_total / count + epsilon_one)


def row_totals(values):
    folded = values[:, :128]
    for k in range(1, values.shape[1] // 128):
        folded = folded + values[:, k * 128 : (k + 1) * 128]
    return jnp.sum(folded.T, axis=0, keepdims=True)


def down_rows(row):
    return jnp.broadcast_to(row, (128, row.shape[1])).T


def rows_kernel(keep, near_one, end, got, g_gate, g_up, pay):
    units = g_gate.shape[1]
    sums = []
    for k, out in enumerate((g_gate, g_up)):
        cols = pl.ds(k * units, units)
        g = add(keep[1, :, cols], near_one[1, :, cols], end[:, cols], got[:, cols])
        out[...] = g
        sums.append(row_totals(g * g))
    block = jnp.concatenate(sums + [jnp.zeros((6, 128), F32)], axis=0)
    for k in range(pay.shape[0]):
        pay[k] = block


def columns_kernel(
    counts, g_gate, g_up, keep, near_one, end, rows, row_gate, row_up, row_down,
    g_down, gate_new, up_new, down_new, pay, gate_out, up_out, down_out, work,
):
    all_units, width = counts
    size = g_down.shape[0]
    g_down[...] = add(keep[size:, :], near_one[size:, :], end[...])
    total = rows[0]
    for k in range(1, rows.shape[0]):
        total = total + rows[k]
    gate_new[...] = moment_step(row_gate[...], total[0:1, :], all_units)
    up_new[...] = moment_step(row_up[...], total[1:2, :], all_units)
    down = g_down[...]
    down_new[...] = moment_step(row_down[...], row_totals(down * down), width)
    gate_out[...] = gate_new[...]
    up_out[...] = up_new[...]
    down_out[...] = down_new[...]
    at = 0
    for g, new in ((g_gate, gate_new), (g_up, up_new), (g_down, down_new)):
        blocks = g.shape[1] // 128
        scale = 1.0 / down_rows(new[...])
        for k in range(blocks):
            value = g[:, k * 128 : (k + 1) * 128]
            square = value * value
            work[pl.ds(at + k, 1), :] = jnp.sum(square, axis=0, keepdims=True)
            work[pl.ds(at + blocks + k, 1), :] = jnp.sum(square * scale, axis=0, keepdims=True)
        at += 2 * blocks
    sums = jnp.concatenate(
        [
            jnp.broadcast_to(jnp.sum(new[...], axis=1, keepdims=True), (1, 128))
            for new in (gate_new, up_new, down_new)
        ]
        + [jnp.zeros((5, 128), F32)],
        axis=0,
    )
    high = sums.astype(BF).astype(F32)
    work[64:72, :] = high
    work[72:80, :] = sums - high
    block = work[...].astype(BF)
    for k in range(pay.shape[0]):
        pay[k] = block


def spread(value):
    return jnp.broadcast_to(
        jnp.sum(jnp.sum(value, axis=0, keepdims=True), axis=1, keepdims=True), (1, 128)
    )


def partial_kernel(width, got, col_gate, col_up, gate_new, up_new, sums, pay, gate_out, up_out):
    total = add(*[got[k] for k in range(got.shape[0])])
    row_sums = total[64:72] + total[72:80]
    gate = moment_step(col_gate[...], total[0:8], width)
    up = moment_step(col_up[...], total[16:24], width)
    gate_new[...] = gate
    up_new[...] = up
    gate_out[...] = gate
    up_out[...] = up
    sums[...] = row_sums
    for k in range(pay.shape[0]):
        pay[k, 0:32, :] = total[32:64]
        pay[k, 32:40, :] = jnp.concatenate(
            [
                spread(total[8:16] / gate),
                spread(total[24:32] / up),
                row_sums[2:3],
                jnp.zeros((5, 128), F32),
            ],
            axis=0,
        )


def update_kernel(
    counts, got, sums, col_down, g_gate, g_up, g_down, row_gate, row_up, row_down, col_gate, col_up,
    gate_out, up_out, down_out, down_new,
):
    all_units, width = counts
    total = got[0]
    for k in range(1, got.shape[0]):
        total = total + got[k]
    down = moment_step(col_down[...], total[0:16], all_units)
    down_new[...] = down
    entries = float(width * all_units)
    work = (
        (gate_out, g_gate, row_gate, col_gate[...], sums[0:1, :] / width, total[32:33]),
        (up_out, g_up, row_up, col_up[...], sums[1:2, :] / width, total[33:34]),
        (down_out, g_down, row_down, down, total[34:35] / all_units, spread(total[16:32] / down)),
    )
    for out, g, row, col, mean, squares in work:
        factor = jnp.sqrt(mean) / jnp.maximum(1.0, jnp.sqrt(mean * squares / entries))
        by_row = lax.rsqrt(down_rows(row[...]))
        by_col = lax.rsqrt(col) * factor
        for k in range(col.shape[0]):
            cols = pl.ds(k * 128, 128)
            out[:, cols] = g[:, cols] * by_row * by_col[k : k + 1, :]


def body(
    tokens, cotangent, w_gate, w_up, w_down, row_gate, col_gate, row_up, col_up, row_down, col_down
):
    rows, width = tokens.shape
    units = w_gate.shape[1]
    all_units = units * 8
    scale = float(rows * 16) ** (-0.5)
    dp, mp = lax.axis_index("dp"), lax.axis_index("mp")
    idx = jnp.stack([dp // 4, (dp // 2) % 2, dp % 2, mp // 2, mp % 2]).astype(jnp.int32)
    swap = dp_shift(dc=1)
    forth, back, across = dp_shift(dz=1), dp_shift(dz=3), dp_shift(dx=1)
    y_forth, y_back, x_across = mp_shift(dy=1), mp_shift(dy=3), mp_shift(dx=1)
    one = 2 * rows * width * units

    cot_peer = lax.ppermute(cotangent, "dp", swap)
    square = near((rows, units), F32)
    gate, tokens, w_gate, w_up = gate_pre(idx, tokens, w_gate, w_up)
    tok_peer = lax.ppermute(tokens, "dp", swap)
    hid = near((2, units // 4, rows), BF)
    act, slope, h_own, h_send = local_kernel(
        "up_pre", up_kernel, idx, [tokens, w_up, gate], [square, square, hid, hid], one
    )
    h_peer = lax.ppermute(h_send, "dp", swap)
    (grad,) = local_kernel(
        "hidden_grad", grad_kernel, None, [cotangent, w_down, act, slope],
        [near((2, rows, units), BF)], one,
        after=(tok_peer, cot_peer),
    )
    grad_peer = lax.ppermute(grad, "dp", swap)

    def down_part(side, after):
        return local_kernel(
            "down", functools.partial(down_kernel, side, scale), None,
            [h_own, h_peer, cotangent, cot_peer], [near((units // 4, width), BF)], one // 2,
            after=after,
        )[0]

    def weight_part(plan, after):
        out = near((2, width // 16, 2 * units), BF)
        return local_kernel(
            "weight", functools.partial(weight_kernel, plan, scale), idx,
            [tokens, tok_peer, grad, grad_peer], [out, out], one, after=after,
        )

    def token_part(plan, after):
        out = near((2, rows, width // 8), BF)
        return local_kernel(
            "token_grad", functools.partial(token_kernel, plan), idx, [grad, w_gate, w_up],
            [out, out], one, after=after,
        )

    tok_r, tok_l = token_part(FIRST, ())
    pair_r, pair_l = weight_part(FIRST, (tok_r,))
    away = down_part(0, (pair_r,))
    pair_a, pair_b = weight_part(SECOND, (away,))
    tok_a, tok_b = token_part(SECOND, (pair_a,))
    own = down_part(1, (tok_a,))

    def middle(parts, got, after):
        out = near(parts[0].shape[1:], BF)
        return local_kernel("middle", middle_kernel, None, [*parts, *got], [out, out], 1000,
                            after=after)

    def crossing(keep, got, end, after):
        out = near(end.shape, BF)
        return local_kernel("crossing", crossing_kernel, None, [keep, got, end], [out], 1000,
                            after=after)[0]

    tok_got = lax.ppermute(tok_r, "mp", y_forth), lax.ppermute(tok_l, "mp", y_back)
    tok_mid = middle((tok_a, tok_b), tok_got, (own,))
    tok_end = lax.ppermute(tok_mid[0], "mp", y_forth), lax.ppermute(tok_mid[1], "mp", y_back)
    pair_got = lax.ppermute(pair_r, "dp", forth), lax.ppermute(pair_l, "dp", back)
    pair_mid = middle((pair_a, pair_b), pair_got, (tok_mid[0],))
    pair_end = lax.ppermute(pair_mid[0], "dp", forth), lax.ppermute(pair_mid[1], "dp", back)
    tok_away = crossing(tok_a, tok_got[1], tok_end[0], (pair_mid[0], tok_end[1]))
    tok_last = lax.ppermute(tok_away, "mp", x_across)
    pair_away = crossing(pair_a, pair_got[1], pair_end[0], (pair_end[1], tok_last))
    pair_last = lax.ppermute(pair_away, "dp", across)
    part = near((units // 8, width), BF)
    down_away, down_keep = local_kernel(
        "down_mix", mix_kernel, None, [own, lax.ppermute(away, "dp", across)], [part] * 2, 1000,
        after=(pair_away,),
    )
    down_got = lax.ppermute(down_away, "dp", dp_pairs(1))
    token_grad, tok_ended = local_kernel(
        "token_end", token_end_kernel, None, [tok_b, tok_got[0], tok_end[1], tok_last],
        [jax.ShapeDtypeStruct((rows, width // 8), BF), near((8, 128), F32)], 1000,
        after=(down_away,),
    )

    shard = near((width // 16, units), F32)
    g_gate, g_up, pay = local_kernel(
        "row_sums", rows_kernel, None,
        [pair_b, pair_got[0], pair_end[1], pair_last],
        [shard, shard, near((8, 8, 128), F32)], 1000, after=(tok_ended,), limit=4,
    )
    (down_mid,) = local_kernel(
        "down_middle", down_middle_kernel, None, [down_keep, down_got],
        [near((units // 16, width), BF)], 1000, after=(g_gate,),
    )
    down_end = lax.ppermute(down_mid, "dp", dp_pairs(3))
    row_got = lax.all_to_all(pay, "mp", 0, 0, tiled=True)

    counts = (all_units, width)
    line = near((1, width // 16), F32)
    short = near((1, units // 16), F32)
    line_out = jax.ShapeDtypeStruct((1, width // 16), F32)
    short_out = jax.ShapeDtypeStruct((1, units // 16), F32)
    g_down, row_gate_new, row_up_new, row_down_new, pay, *rows_out, _ = local_kernel(
        "column_sums", functools.partial(columns_kernel, counts), None,
        [
            g_gate, g_up, down_keep, down_got, down_end, row_got,
            row_gate.reshape(1, -1), row_up.reshape(1, -1), row_down.reshape(1, -1),
        ],
        [near((units // 16, width), F32), line, line, short, near((16, 80, 128), BF),
         line_out, line_out, short_out, near((80, 128), F32)],
        1000, limit=4,
    )
    col_got = lax.all_to_all(pay, "dp", 0, 0, tiled=True)

    lines = near((units // 128, 128), F32)
    lines_out = jax.ShapeDtypeStruct((units // 128, 128), F32)
    col_gate_new, col_up_new, sums, pay, *cols_out = local_kernel(
        "partial_sums", functools.partial(partial_kernel, width), None,
        [col_got, col_gate.reshape(-1, 128), col_up.reshape(-1, 128)],
        [lines, lines, near((8, 128), F32), near((8, 40, 128), F32), lines_out, lines_out], 1000, limit=4,
    )
    last = lax.all_to_all(pay, "mp", 0, 0, tiled=True)
    update_gate, update_up, update_down, col_down_new = local_kernel(
        "updates", functools.partial(update_kernel, counts), None,
        [
            last, sums, col_down.reshape(-1, 128), g_gate, g_up, g_down,
            row_gate_new, row_up_new, row_down_new, col_gate_new, col_up_new,
        ],
        [
            jax.ShapeDtypeStruct((width // 16, units), F32),
            jax.ShapeDtypeStruct((width // 16, units), F32),
            jax.ShapeDtypeStruct((units // 16, width), F32),
            jax.ShapeDtypeStruct((width // 128, 128), F32),
        ],
        1000, limit=8,
    )
    return (
        token_grad,
        update_gate,
        update_up,
        update_down,
        rows_out[0].reshape(-1),
        cols_out[0].reshape(-1),
        rows_out[1].reshape(-1),
        cols_out[1].reshape(-1),
        rows_out[2].reshape(-1),
        col_down_new.reshape(-1),
    )


def solution(mesh):
    in_specs = (
        P("dp", None),
        P("dp", None),
        P(None, "mp"),
        P(None, "mp"),
        P("mp", None),
        P("dp"),
        P("mp"),
        P("dp"),
        P("mp"),
        P(("mp", "dp")),
        P(),
    )
    out_specs = (
        P("dp", "mp"),
        P("dp", "mp"),
        P("dp", "mp"),
        P(("mp", "dp"), None),
        P("dp"),
        P("mp"),
        P("dp"),
        P("mp"),
        P(("mp", "dp")),
        P(),
    )
    return jax.shard_map(body, mesh=mesh, in_specs=in_specs, out_specs=out_specs, check_vma=False)
```
